256 devices in a mesh: group: 8 (over z), dom: 32 (over y, x, core).
Axes of the slice: x: 4, y: 4, z: 8, core: 2. Of those that a mesh axis runs over, the one named last changes fastest.
Arguments:
- pressure_old: float32 [1048576], P(('group', 'dom')), may hold values from -6 to 6
- source_term: float32 [1048576], P(('group', 'dom')), may hold values from -36 to 36
- diagonal: float32 [1048576], P(('group', 'dom')), may hold values from 6.5 to 7.5
- face_coeffs: float32 [6, 1048576], P(None, ('group', 'dom')), may hold values from 0.1 to 0.9
- neighbours: int32 [6, 1048576], P(None, ('group', 'dom')), may hold values from 0 to 8191
- export_cells: int32 [4, 262144], P(None, ('group', 'dom')), may hold values from 0 to 4095
- fluid_velocity: float32 [3, 1048576], P(None, ('group', 'dom')), may hold values from -6 to 6
- parcel_velocity: float32 [3, 262144], P(None, ('group', 'dom')), may hold values from -6 to 6
- drag_rate: float32 [262144], P(('group', 'dom')), may hold values from 0.05 to 1
- parcel_owner: int32 [262144], P(('group', 'dom')), may hold values from 0 to 31, as said below
- parcel_cells: int32 [8, 262144], P(None, ('group', 'dom')), may hold values from 0 to 4095
- interp_weights: float32 [8, 262144], P(None, ('group', 'dom')), may hold values from 0 to 0.25
- grad_weights: float32 [3, 8, 262144], P(None, None, ('group', 'dom')), may hold values from -3 to 3
Outputs:
- pressure: float32 [1048576], P(('group', 'dom'))
- parcel_new: float32 [3, 262144], P(None, ('group', 'dom'))
- momentum_source: float32 [3, 1048576], P(None, ('group', 'dom'))
The draws below stay inside these ranges and needn't reach their ends.
Inputs may be any that keep to these rules, and one draw needn't show every extreme that they name: `parcel_owner`: A parcel's cells lie in its own group; in every group one partition is named exactly 128 times by the parcels of each device of the group, and no partition is named more than 128 times by the parcels of one device. `neighbours`: values under 4096 are the device's own cells; 4096 + d * 1024 + f is entry f of the cells exported by the neighbour in direction d. `export_cells`: local cell indices; repeats may occur.
All inputs are finite; a program needn't handle non-finite values.
Results may differ from the reference program's by a relative error of at most 0.00002.
Values sent between devices are 32-bit elements; how exact they have to be, the bound alone decides.
No kernel may reach another device: no remote copies, remote signals or barrier semaphores. Data moves between devices by JAX's collectives and lax.ppermute only.
A program may use at most 192 MiB of HBM per device.

```python
import math
import jax
import jax.numpy as jnp

CELLS_DEV = 4096
FACE = 1024
NBR = 6
K = 8
PAR_DEV = 1024
ITERS = 2
CELLS = 1048576
PARCELS = 262144
CAP = 128
N_GROUP = 8
N_DOM = 32


def draw_parcel_owner(key, part):
    others = (N_DOM - 1) * CAP

    def one_device(device):
        group_key = jax.random.fold_in(jax.random.fold_in(key, 21), device // N_DOM)
        busiest = jax.random.randint(group_key, (), 0, N_DOM)
        device_key = jax.random.fold_in(jax.random.fold_in(key, 22), device)
        tickets = jnp.arange(others, dtype=jnp.int32) // CAP
        tickets = jnp.where(tickets >= busiest, tickets + 1, tickets)
        chosen = jax.random.permutation(jax.random.fold_in(device_key, 1), tickets)[:PAR_DEV - CAP]
        owners = jnp.concatenate([jnp.full((CAP,), busiest, jnp.int32), chosen.astype(jnp.int32)])
        return jax.random.permutation(jax.random.fold_in(device_key, 2), owners)
    return jax.vmap(one_device)(jnp.arange(N_GROUP * N_DOM, dtype=jnp.int32)).reshape(-1)


def set_ends(values, stream_key, low, high):
    place = [jax.random.randint(jax.random.fold_in(stream_key, axis), (), 0, length) for axis, length in enumerate(values.shape)]
    longest = values.shape.index(max(values.shape))
    next_to = place[:longest] + [(place[longest] + 1) % values.shape[longest]] + place[longest + 1:]
    return values.at[tuple(place)].set(low).at[tuple(next_to)].set(high)


def block_levels(own_key, shape, shards, least, largest):
    def one(dim, parts):
        draws = jax.random.uniform(jax.random.fold_in(jax.random.fold_in(own_key, 6), dim), (parts,), jnp.float32, least / len(shards), largest / len(shards))
        return jnp.repeat(jnp.exp(draws), shape[dim] // parts).reshape((-1,) + (1,) * (len(shape) - dim - 1))

    loudness = one(*shards[0])
    for cut in shards[1:]:
        loudness = loudness * one(*cut)
    return loudness


def noise(stream_key, extent, width, reach, shards=(), held_as=jnp.bfloat16):
    gain = block_levels(stream_key, extent, shards, -0.22, 0.18) if shards else 1.0
    drawn = jax.random.normal(stream_key, extent, jnp.float32) * width * gain
    return jnp.minimum(jnp.maximum(drawn, -reach), reach).astype(held_as)


def setup_inputs(seed: int = 0) -> dict:
    key_list = jax.random.split(jax.random.key(seed), 14)
    return {
        "pressure_old": noise(key_list[0], (CELLS,), 1.0, 6.0, ((0, 256),), jnp.float32),
        "source_term": noise(key_list[1], (CELLS,), 6.0, 36.0, ((0, 256),), jnp.float32),
        "diagonal": jnp.clip(6.5 + 1.0 * jax.random.uniform(key_list[2], (CELLS,), jnp.float32) ** block_levels(key_list[2], (CELLS,), ((0, 256),), -0.2, 0.2), 6.5, 7.5),
        "face_coeffs": jnp.clip(jnp.exp(math.log(0.9) - 2.1972245 * jax.random.uniform(key_list[3], (NBR, CELLS), jnp.float32) ** block_levels(key_list[3], (NBR, CELLS), ((1, 256),), -0.2, 0.2)), 0.1, 0.9),
        "neighbours": set_ends(jax.random.randint(key_list[4], (NBR, CELLS), 0, CELLS_DEV + 4 * FACE), jax.random.fold_in(key_list[4], 1), 0, (CELLS_DEV + 4 * FACE) - 1).astype(jnp.int32),
        "export_cells": set_ends(jax.random.randint(key_list[5], (4, FACE * N_GROUP * N_DOM), 0, CELLS_DEV), jax.random.fold_in(key_list[5], 1), 0, CELLS_DEV - 1).astype(jnp.int32),
        "fluid_velocity": noise(key_list[6], (3, CELLS), 1.0, 6.0, ((1, 256),), jnp.float32),
        "parcel_velocity": noise(key_list[7], (3, PARCELS), 1.0, 6.0, ((1, 256),), jnp.float32),
        "drag_rate": jnp.clip(jnp.exp(math.log(1.0) - 2.9957323 * jax.random.uniform(key_list[8], (PARCELS,), jnp.float32) ** block_levels(key_list[8], (PARCELS,), ((0, 256),), -0.2, 0.2)), 0.05, 1.0),
        "parcel_owner": draw_parcel_owner(jax.random.fold_in(key_list[13], 71), 0),
        "parcel_cells": set_ends(jax.random.randint(key_list[10], (K, PARCELS), 0, CELLS_DEV), jax.random.fold_in(key_list[10], 1), 0, CELLS_DEV - 1).astype(jnp.int32),
        "interp_weights": jnp.clip(0.25 * jax.random.uniform(key_list[11], (K, PARCELS), jnp.float32) ** block_levels(key_list[11], (K, PARCELS), ((1, 256),), -0.2, 0.2), 0.0, 0.25),
        "grad_weights": noise(key_list[12], (3, K, PARCELS), 0.5, 3.0, ((2, 256),), jnp.float32),
    }


CENTRE = 7.0
HALF_WIDTH = 4.0
LOADING = 8.0


def apply_matrix(vector, diagonal, face_coeffs, neighbours, export_cells):
    devices = N_GROUP * N_DOM
    local = vector.reshape(devices, CELLS_DEV)
    offsets = jnp.repeat(jnp.arange(devices, dtype=jnp.int32) * CELLS_DEV, FACE)
    exported = vector[export_cells + offsets[None, :]]
    exported = exported.reshape(4, N_GROUP, N_DOM, FACE)
    zeros_row = jnp.zeros((1, N_DOM, FACE), jnp.float32)
    from_lower = jnp.roll(exported[0], 1, axis=1)
    from_upper = jnp.roll(exported[1], -1, axis=1)
    from_below = jnp.concatenate([zeros_row, exported[2][:-1]], axis=0)
    from_above = jnp.concatenate([exported[3][1:], zeros_row], axis=0)
    received = jnp.stack([from_lower, from_upper, from_below, from_above], axis=2).reshape(devices, 4 * FACE)
    extended = jnp.concatenate([local, received], axis=1)
    coeffs = face_coeffs.reshape(NBR, devices, CELLS_DEV)
    links = neighbours.reshape(NBR, devices, CELLS_DEV)
    result = diagonal.reshape(devices, CELLS_DEV) * local
    for column in range(NBR):
        result = result - coeffs[column] * jnp.take_along_axis(extended, links[column], axis=1)
    return result.reshape(-1)


def reference(pressure_old, source_term, diagonal, face_coeffs, neighbours, export_cells, fluid_velocity, parcel_velocity, drag_rate, parcel_owner, parcel_cells, interp_weights, grad_weights):
    def operate(vector):
        return apply_matrix(vector, diagonal, face_coeffs, neighbours, export_cells)

    sigma = CENTRE / HALF_WIDTH
    rho_now = 1.0 / sigma
    iterate = pressure_old
    residual = source_term - operate(pressure_old)
    direction = residual / CENTRE
    for iteration in range(ITERS):
        iterate = iterate + direction
        if iteration + 1 < ITERS:
            residual = residual - operate(direction)
            rho_next = 1.0 / (2.0 * sigma - rho_now)
            direction = rho_next * rho_now * direction + (2.0 * rho_next / HALF_WIDTH) * residual
            rho_now = rho_next
    pressure = iterate

    group_of = jnp.arange(PARCELS, dtype=jnp.int32) // (PAR_DEV * N_DOM)
    cell_ids = ((group_of * N_DOM + parcel_owner) * CELLS_DEV)[None, :] + parcel_cells
    fluid_at = jnp.sum(interp_weights[None] * fluid_velocity[:, cell_ids], axis=1)
    grad_at = jnp.sum(grad_weights * pressure[cell_ids][None], axis=1)
    moved = parcel_velocity + drag_rate[None] * (fluid_at - parcel_velocity)
    parcel_new = moved - grad_at
    reaction = LOADING * interp_weights[None] * (drag_rate[None] * (parcel_velocity - fluid_at))[:, None, :]
    momentum_source = jnp.zeros((3, CELLS), jnp.float32).at[:, cell_ids].add(reaction)
    return (pressure, parcel_new, momentum_source)
```

```python
import jax
import jax.numpy as jnp
from jax import lax
from jax.experimental import pallas as pl
from jax.experimental.pallas import tpu as pltpu
from jax.sharding import PartitionSpec as P

CENTRE = 7.0
HALF_WIDTH = 4.0
LOADING = 8.0
SIGMA = CENTRE / HALF_WIDTH
RHO_FIRST = 1.0 / SIGMA
RHO_NEXT = 1.0 / (2.0 * SIGMA - RHO_FIRST)

CELLS = 4096
LANES = 128
ROWS = CELLS // LANES
FACE = 1024
FACE_ROWS = FACE // LANES
NBR = 6
K = 8
PARCELS = 1024
CHUNKS = PARCELS // LANES
OWNERS = 32
CAP = 128
SENT = 48

F32 = jnp.float32
BF16 = jnp.bfloat16
I32 = jnp.int32


def pick(row, lanes):
    return jnp.take_along_axis(row, lanes, axis=1, mode="promise_in_bounds")


def wide(row, height):
    return jnp.broadcast_to(row, (height, LANES))


def look_up(tables, index):
    height = index.shape[0]
    high = lax.shift_right_logical(index, 7)
    low = lax.bitwise_and(index, 127)
    found = [jnp.zeros((height, LANES), F32) for _ in tables]
    for r in range(len(tables[0])):
        here = high == r
        for c, table in enumerate(tables):
            found[c] = jnp.where(here, pick(wide(table[r](), height), low), found[c])
    return found


def rows_of(ref, count):
    return [lambda r=r: ref[r : r + 1, :] for r in range(count)]


def write_exports(field_ref, export_ref, outs):
    for t in range(FACE_ROWS):
        index = export_ref[:, t * LANES : (t + 1) * LANES]
        (found,) = look_up([rows_of(field_ref, ROWS)], index)
        for d in range(4):
            outs[d][t : t + 1, :] = found[d : d + 1, :]


def export_kernel(field_ref, export_ref, *outs):
    write_exports(field_ref, export_ref, outs)


def multiply(vector_ref, got_refs, diagonal_ref, coeff_ref, neighbour_ref, halo_ref, out_ref):
    group = lax.axis_index("group")
    last = lax.axis_size("group") - 1
    for d in range(4):
        value = got_refs[d][...]
        if d == 2:
            value = jnp.where(group > 0, value, 0.0)
        if d == 3:
            value = jnp.where(group < last, value, 0.0)
        halo_ref[d * FACE_ROWS : (d + 1) * FACE_ROWS, :] = value
    table = rows_of(vector_ref, ROWS) + rows_of(halo_ref, 4 * FACE_ROWS)
    for t in range(ROWS):
        cut = slice(t * LANES, (t + 1) * LANES)
        (found,) = look_up([table], neighbour_ref[:, cut])
        linked = jnp.sum(coeff_ref[:, cut] * found, axis=0, keepdims=True)
        out_ref[t : t + 1, :] = diagonal_ref[t : t + 1, :] * vector_ref[t : t + 1, :] - linked


def first_kernel(
    pressure_ref, got0, got1, got2, got3, source_ref, diagonal_ref, coeff_ref, neighbour_ref,
    export_ref, residual_ref, direction_ref, out0, out1, out2, out3, halo_ref, product_ref,
):
    multiply(
        pressure_ref, (got0, got1, got2, got3), diagonal_ref, coeff_ref, neighbour_ref,
        halo_ref, product_ref,
    )
    residual = source_ref[...] - product_ref[...]
    residual_ref[...] = residual
    direction_ref[...] = residual / CENTRE
    write_exports(direction_ref, export_ref, (out0, out1, out2, out3))


def second_kernel(
    direction_ref, got0, got1, got2, got3, pressure_ref, residual_ref, diagonal_ref, coeff_ref,
    neighbour_ref, parcel_ref, moved_ref, out_ref, updated_ref, halo_ref, product_ref,
):
    multiply(
        direction_ref, (got0, got1, got2, got3), diagonal_ref, coeff_ref, neighbour_ref,
        halo_ref, product_ref,
    )
    direction = direction_ref[...]
    residual = residual_ref[...] - product_ref[...]
    iterate = pressure_ref[...] + direction
    direction = RHO_NEXT * RHO_FIRST * direction + (2.0 * RHO_NEXT / HALF_WIDTH) * residual
    out_ref[...] = iterate + direction
    table = rows_of(out_ref, ROWS)
    for s in range(OWNERS):
        (found,) = look_up([table], parcel_ref[s, 8:16, :].astype(I32))
        for c in range(3):
            weights = parcel_ref[s, 16 + 8 * c : 24 + 8 * c, :]
            gradient = jnp.sum(weights * found, axis=0, keepdims=True)
            updated_ref[s, c : c + 1, :] = moved_ref[s, c : c + 1, :] - gradient
        updated_ref[s, 3:4, :] = jnp.zeros((1, LANES), F32)


def slot_kernel(owner_ref, cells_ref, weight_ref, grad_ref, velocity_ref, rate_ref, place_ref, sent_ref):
    owners = lax.broadcasted_iota(I32, (OWNERS, LANES), 0)
    lanes = lax.broadcasted_iota(I32, (OWNERS, LANES), 1)
    chosen = [owners == wide(owner_ref[j : j + 1, :], OWNERS) for j in range(CHUNKS)]
    stacked = jnp.concatenate([c.astype(F32).astype(BF16) for c in chosen], axis=0)
    row = lax.broadcasted_iota(I32, (LANES, 2 * LANES), 0)
    column = lax.broadcasted_iota(I32, (LANES, 2 * LANES), 1)
    before = ((row < column) | (column >= LANES)).astype(F32).astype(BF16)
    counts = jnp.dot(stacked, before, preferred_element_type=F32)
    carried = jnp.zeros((OWNERS, LANES), F32)
    ranks = []
    for j in range(CHUNKS):
        part = counts[j * OWNERS : (j + 1) * OWNERS]
        rank = jnp.where(chosen[j], part[:, :LANES] + carried, 0.0)
        ranks.append(jnp.sum(rank, axis=0, keepdims=True))
        carried = carried + part[:, LANES:]
        place_ref[j : j + 1, :] = owner_ref[j : j + 1, :] * CAP + ranks[j].astype(I32)
    slots = lax.broadcasted_iota(I32, (CAP, LANES), 0).astype(F32)
    at_rank = jnp.concatenate(
        [(slots == wide(ranks[j], CAP)).astype(F32).astype(BF16) for j in range(CHUNKS)], axis=1
    )
    lane_of = jnp.concatenate(
        [jnp.where(c, lanes.astype(F32), 0.0).astype(BF16) for c in chosen], axis=1
    )
    chunk_of = jnp.concatenate(
        [jnp.where(c, F32(j + 1), 0.0).astype(BF16) for j, c in enumerate(chosen)], axis=1
    )
    found = lax.dot_general(
        jnp.concatenate([lane_of, chunk_of], axis=0), at_rank, (((1,), (1,)), ((), ())),
        preferred_element_type=F32,
    ).astype(I32)
    for o in range(OWNERS):
        low = wide(found[o : o + 1], 8)
        high = wide(found[OWNERS + o : OWNERS + o + 1], 8)
        here = [high == j + 1 for j in range(CHUNKS)]

        def place(group, ref, height=8):
            value = jnp.zeros((height, LANES), F32)
            for j in range(CHUNKS):
                cut = slice(j * LANES, (j + 1) * LANES)
                part = ref[:, cut] if group is None else ref[group, :, cut]
                value = jnp.where(here[j][:height], pick(part.astype(F32), low[:height]), value)
            return value

        sent_ref[o, 0:8, :] = place(None, weight_ref)
        sent_ref[o, 8:16, :] = place(None, cells_ref)
        for c in range(3):
            sent_ref[o, 16 + 8 * c : 24 + 8 * c, :] = place(c, grad_ref)
        sent_ref[o, 40:43, :] = place(None, velocity_ref, 3)
        value = jnp.zeros((8, LANES), F32)
        for j in range(CHUNKS):
            value = jnp.where(here[j], pick(wide(rate_ref[j : j + 1, :], 8), low), value)
        sent_ref[o, 43:44, :] = value[:1]
        sent_ref[o, 44:48, :] = jnp.zeros((4, LANES), F32)


def fluid_kernel(fluid_ref, parcel_ref, moved_ref, force_ref):
    tables = [
        [lambda c=c, r=r: fluid_ref[c : c + 1, r * LANES : (r + 1) * LANES] for r in range(ROWS)]
        for c in range(3)
    ]
    for s in range(OWNERS):
        found = look_up(tables, parcel_ref[s, 8:16, :].astype(I32))
        weights = parcel_ref[s, 0:8, :]
        rate = parcel_ref[s, 43:44, :]
        for c in range(3):
            velocity = parcel_ref[s, 40 + c : 41 + c, :]
            fluid_at = jnp.sum(weights * found[c], axis=0, keepdims=True)
            moved_ref[s, c : c + 1, :] = velocity + rate * (fluid_at - velocity)
            force_ref[s, c : c + 1, :] = rate * (velocity - fluid_at)
        moved_ref[s, 3:4, :] = jnp.zeros((1, LANES), F32)
        force_ref[s, 3:4, :] = jnp.zeros((1, LANES), F32)


def scatter_kernel(parcel_ref, force_ref, out_ref, total_ref):
    rows = lax.broadcasted_iota(I32, (ROWS, LANES), 0)
    columns = lax.broadcasted_iota(I32, (LANES, LANES), 0)
    total_ref[...] = jnp.zeros_like(total_ref)

    def step(s, carry):
        cells = parcel_ref[s, 8:16, :].astype(I32)
        high = lax.shift_right_logical(cells, 7)
        low = lax.bitwise_and(cells, 127)
        weights = LOADING * parcel_ref[s, 0:8, :]
        parts = []
        for c in range(3):
            value = weights * force_ref[s, c : c + 1, :]
            top = value.astype(BF16)
            parts.append(top.astype(F32))
            parts.append((value - top.astype(F32)).astype(BF16).astype(F32))
        left, right = [], []
        for k in range(K):
            here = rows == wide(high[k : k + 1], ROWS)
            left.append(
                jnp.concatenate(
                    [jnp.where(here, wide(p[k : k + 1], ROWS), 0.0).astype(BF16) for p in parts],
                    axis=0,
                )
            )
            right.append((columns == wide(low[k : k + 1], LANES)).astype(F32).astype(BF16))
        total_ref[...] += lax.dot_general(
            jnp.concatenate(left, axis=1), jnp.concatenate(right, axis=1),
            (((1,), (1,)), ((), ())), preferred_element_type=F32,
        )
        return carry

    lax.fori_loop(0, OWNERS, step, 0)
    for c in range(3):
        both = (
            total_ref[2 * c * ROWS : (2 * c + 1) * ROWS, :]
            + total_ref[(2 * c + 1) * ROWS : (2 * c + 2) * ROWS, :]
        )
        for r in range(ROWS):
            out_ref[c : c + 1, r * LANES : (r + 1) * LANES] = both[r : r + 1]


def return_kernel(place_ref, updated_ref, out_ref):
    tables = [[lambda c=c, o=o: updated_ref[o, c : c + 1, :] for o in range(OWNERS)] for c in range(3)]
    found = look_up(tables, place_ref[...])
    for c in range(3):
        for j in range(CHUNKS):
            out_ref[c : c + 1, j * LANES : (j + 1) * LANES] = found[c][j : j + 1]


def shape(*dims, dtype=F32):
    return jax.ShapeDtypeStruct(dims, dtype)


def exchange(faces):
    count, groups = lax.axis_size("dom"), lax.axis_size("group")
    up = [(i, (i + 1) % count) for i in range(count)]
    over = [(i, (i + 1) % groups) for i in range(groups)]
    down = [(b, a) for a, b in up]
    under = [(b, a) for a, b in over]
    return (
        lax.ppermute(faces[0], "dom", up),
        lax.ppermute(faces[1], "dom", down),
        lax.ppermute(faces[2], "group", over),
        lax.ppermute(faces[3], "group", under),
    )


def call(kernel, outs, flops, scratch=()):
    return pl.pallas_call(
        kernel,
        out_shape=outs,
        scratch_shapes=list(scratch),
        compiler_params=pltpu.CompilerParams(vmem_limit_bytes=32 * 1024 * 1024),
        cost_estimate=pl.CostEstimate(flops=flops, bytes_accessed=400000, transcendentals=0),
    )


def per_device(
    pressure_old, source_term, diagonal, face_coeffs, neighbours, export_cells, fluid_velocity,
    parcel_velocity, drag_rate, parcel_owner, parcel_cells, interp_weights, grad_weights,
):
    pressure_old = pressure_old.reshape(ROWS, LANES)
    source_term = source_term.reshape(ROWS, LANES)
    diagonal = diagonal.reshape(ROWS, LANES)
    face = shape(FACE_ROWS, LANES)
    field = shape(ROWS, LANES)
    halo = (pltpu.VMEM((4 * FACE_ROWS, LANES), F32), pltpu.VMEM((ROWS, LANES), F32))

    faces = call(export_kernel, (face,) * 4, 10**6)(pressure_old, export_cells)
    place, sent = call(
        slot_kernel, (shape(CHUNKS, LANES, dtype=I32), shape(OWNERS, SENT, CAP)), 10**8
    )(
        parcel_owner.reshape(CHUNKS, LANES), parcel_cells, interp_weights, grad_weights,
        parcel_velocity, drag_rate.reshape(CHUNKS, LANES),
    )
    parcels = lax.all_to_all(sent, "dom", split_axis=0, concat_axis=0, tiled=True)
    got = exchange(faces)
    residual, direction, *faces = call(first_kernel, (field, field) + (face,) * 4, 10**8, halo)(
        pressure_old, *got, source_term, diagonal, face_coeffs, neighbours, export_cells
    )
    got = exchange(faces)
    moved, force = call(fluid_kernel, (shape(OWNERS, 4, CAP),) * 2, 10**9)(fluid_velocity, parcels)
    iterate, updated = call(second_kernel, (field, shape(OWNERS, 4, CAP)), 10**8, halo)(
        direction, *got, pressure_old, residual, diagonal, face_coeffs, neighbours, parcels, moved
    )
    returned = lax.all_to_all(updated, "dom", split_axis=0, concat_axis=0, tiled=True)
    momentum_source = call(
        scatter_kernel, shape(3, CELLS), 2 * 10**9, (pltpu.VMEM((6 * ROWS, LANES), F32),)
    )(parcels, force)
    parcel_new = call(return_kernel, shape(3, PARCELS), 10**6)(place, returned)
    return (iterate.reshape(CELLS), parcel_new, momentum_source)


def solution(mesh):
    whole = ("group", "dom")
    flat, rows = P(whole), P(None, whole)
    return jax.shard_map(
        per_device,
        mesh=mesh,
        in_specs=(
            flat, flat, flat, rows, rows, rows, rows, rows, flat, flat, rows, rows,
            P(None, None, whole),
        ),
        out_specs=(flat, rows, rows),
        check_vma=False,
    )
```

```python
import jax
import jax.numpy as jnp
from jax import lax
from jax.experimental import pallas as pl
from jax.experimental.pallas import tpu as pltpu
from jax.sharding import PartitionSpec as P

CENTRE = 7.0
HALF_WIDTH = 4.0
LOADING = 8.0
SIGMA = CENTRE / HALF_WIDTH
RHO_FIRST = 1.0 / SIGMA
RHO_NEXT = 1.0 / (2.0 * SIGMA - RHO_FIRST)

CELLS = 4096
LANES = 128
ROWS = CELLS // LANES
FACE = 1024
FACE_ROWS = FACE // LANES
NBR = 6
K = 8
PARCELS = 1024
CHUNKS = PARCELS // LANES
OWNERS = 32
CAP = 128
SENT = 24

F32 = jnp.float32
BF16 = jnp.bfloat16
I32 = jnp.int32


def pick(row, lanes):
    return jnp.take_along_axis(row, lanes, axis=1, mode="promise_in_bounds")


def wide(row, height):
    return jnp.broadcast_to(row, (height, LANES))


def look_up(tables, index):
    height = index.shape[0]
    high = lax.shift_right_logical(index, 7)
    low = lax.bitwise_and(index, 127)
    found = [jnp.zeros((height, LANES), F32) for _ in tables]
    for r in range(len(tables[0])):
        here = high == r
        for c, table in enumerate(tables):
            found[c] = jnp.where(here, pick(wide(table[r](), height), low), found[c])
    return found


def rows_of(ref, count):
    return [lambda r=r: ref[r : r + 1, :] for r in range(count)]


def is_even(axis):
    return lax.rem(lax.axis_index(axis), 2) == 0


def write_exports(field_ref, export_ref, face_ref, outs):
    for t in range(FACE_ROWS):
        index = export_ref[:, t * LANES : (t + 1) * LANES]
        (found,) = look_up([rows_of(field_ref, ROWS)], index)
        for d in range(4):
            face_ref[d, t : t + 1, :] = found[d : d + 1]
    for axis, d in (("dom", 0), ("group", 2)):
        even = is_even(axis)
        outs[d][...] = jnp.where(even, face_ref[d], face_ref[d + 1])
        outs[d + 1][...] = jnp.where(even, face_ref[d + 1], face_ref[d])


def export_kernel(field_ref, export_ref, out0, out1, out2, out3, face_ref):
    write_exports(field_ref, export_ref, face_ref, (out0, out1, out2, out3))


def multiply(vector_ref, got_refs, diagonal_ref, coeff_ref, neighbour_ref, halo_ref, out_ref):
    group = lax.axis_index("group")
    last = lax.axis_size("group") - 1
    for axis, d in (("dom", 0), ("group", 2)):
        even = is_even(axis)
        below = jnp.where(even, got_refs[d + 1][...], got_refs[d][...])
        above = jnp.where(even, got_refs[d][...], got_refs[d + 1][...])
        if axis == "group":
            below = jnp.where(group > 0, below, 0.0)
            above = jnp.where(group < last, above, 0.0)
        halo_ref[d * FACE_ROWS : (d + 1) * FACE_ROWS, :] = below
        halo_ref[(d + 1) * FACE_ROWS : (d + 2) * FACE_ROWS, :] = above
    table = rows_of(vector_ref, ROWS) + rows_of(halo_ref, 4 * FACE_ROWS)
    for t in range(0, ROWS, 4):
        cuts = [slice(u * LANES, (u + 1) * LANES) for u in range(t, t + 4)]
        (found,) = look_up([table], jnp.concatenate([neighbour_ref[:, cut] for cut in cuts], axis=0))
        for u, cut in enumerate(cuts):
            part = coeff_ref[:, cut] * found[NBR * u : NBR * (u + 1)]
            linked = jnp.sum(part, axis=0, keepdims=True)
            row = slice(t + u, t + u + 1)
            out_ref[row, :] = diagonal_ref[row, :] * vector_ref[row, :] - linked


def first_kernel(
    pressure_ref, got0, got1, got2, got3, source_ref, diagonal_ref, coeff_ref, neighbour_ref,
    export_ref, residual_ref, direction_ref, out0, out1, out2, out3, halo_ref, product_ref, face_ref,
):
    multiply(
        pressure_ref, (got0, got1, got2, got3), diagonal_ref, coeff_ref, neighbour_ref,
        halo_ref, product_ref,
    )
    residual = source_ref[...] - product_ref[...]
    residual_ref[...] = residual
    direction_ref[...] = residual / CENTRE
    write_exports(direction_ref, export_ref, face_ref, (out0, out1, out2, out3))


def second_kernel(
    direction_ref, got0, got1, got2, got3, pressure_ref, residual_ref, diagonal_ref, coeff_ref,
    neighbour_ref, parcel_ref, moved_ref, out_ref, answer_ref, halo_ref, product_ref,
):
    multiply(
        direction_ref, (got0, got1, got2, got3), diagonal_ref, coeff_ref, neighbour_ref,
        halo_ref, product_ref,
    )
    direction = direction_ref[...]
    residual = residual_ref[...] - product_ref[...]
    iterate = pressure_ref[...] + direction
    direction = RHO_NEXT * RHO_FIRST * direction + (2.0 * RHO_NEXT / HALF_WIDTH) * residual
    out_ref[...] = iterate + direction
    table = rows_of(out_ref, ROWS)
    for s in range(OWNERS):
        (found,) = look_up([table], parcel_ref[s, 8:16, :].astype(I32))
        answer_ref[s, 0:8, :] = found
        answer_ref[s, 8:16, :] = moved_ref[s]


def slot_kernel(owner_ref, cells_ref, weight_ref, velocity_ref, rate_ref, place_ref, sent_ref):
    owners = lax.broadcasted_iota(I32, (OWNERS, LANES), 0)
    lanes = lax.broadcasted_iota(I32, (OWNERS, LANES), 1)
    chosen = [owners == wide(owner_ref[j : j + 1, :], OWNERS) for j in range(CHUNKS)]
    stacked = jnp.concatenate([c.astype(F32).astype(BF16) for c in chosen], axis=0)
    row = lax.broadcasted_iota(I32, (LANES, 2 * LANES), 0)
    column = lax.broadcasted_iota(I32, (LANES, 2 * LANES), 1)
    before = ((row < column) | (column >= LANES)).astype(F32).astype(BF16)
    counts = jnp.dot(stacked, before, preferred_element_type=F32)
    carried = jnp.zeros((OWNERS, LANES), F32)
    ranks = []
    for j in range(CHUNKS):
        part = counts[j * OWNERS : (j + 1) * OWNERS]
        rank = jnp.where(chosen[j], part[:, :LANES] + carried, 0.0)
        ranks.append(jnp.sum(rank, axis=0, keepdims=True))
        carried = carried + part[:, LANES:]
        place_ref[j : j + 1, :] = owner_ref[j : j + 1, :] * CAP + ranks[j].astype(I32)
    slots = lax.broadcasted_iota(I32, (CAP, LANES), 0).astype(F32)
    at_rank = jnp.concatenate(
        [(slots == wide(ranks[j], CAP)).astype(F32).astype(BF16) for j in range(CHUNKS)], axis=1
    )
    lane_of = jnp.concatenate(
        [jnp.where(c, lanes.astype(F32), 0.0).astype(BF16) for c in chosen], axis=1
    )
    chunk_of = jnp.concatenate(
        [jnp.where(c, F32(j + 1), 0.0).astype(BF16) for j, c in enumerate(chosen)], axis=1
    )
    found = lax.dot_general(
        jnp.concatenate([lane_of, chunk_of], axis=0), at_rank, (((1,), (1,)), ((), ())),
        preferred_element_type=F32,
    ).astype(I32)
    for o in range(OWNERS):
        low = wide(found[o : o + 1], 8)
        high = wide(found[OWNERS + o : OWNERS + o + 1], 8)
        here = [high == j + 1 for j in range(CHUNKS)]

        def place(ref, height=8):
            value = jnp.zeros((height, LANES), F32)
            for j in range(CHUNKS):
                part = ref[:, j * LANES : (j + 1) * LANES].astype(F32)
                value = jnp.where(here[j][:height], pick(part, low[:height]), value)
            return value

        sent_ref[o, 0:8, :] = place(weight_ref)
        sent_ref[o, 8:16, :] = place(cells_ref)
        sent_ref[o, 16:19, :] = place(velocity_ref, 3)
        value = jnp.zeros((8, LANES), F32)
        for j in range(CHUNKS):
            value = jnp.where(here[j], pick(wide(rate_ref[j : j + 1, :], 8), low), value)
        sent_ref[o, 19:24, :] = jnp.concatenate([value[:1], jnp.zeros((4, LANES), F32)], axis=0)


def fluid_kernel(fluid_ref, parcel_ref, moved_ref, force_ref):
    tables = [
        [lambda c=c, r=r: fluid_ref[c : c + 1, r * LANES : (r + 1) * LANES] for r in range(ROWS)]
        for c in range(3)
    ]
    for s in range(OWNERS):
        found = look_up(tables, parcel_ref[s, 8:16, :].astype(I32))
        weights = parcel_ref[s, 0:8, :]
        rate = parcel_ref[s, 19:20, :]
        for c in range(3):
            velocity = parcel_ref[s, 16 + c : 17 + c, :]
            fluid_at = jnp.sum(weights * found[c], axis=0, keepdims=True)
            moved_ref[s, c : c + 1, :] = velocity + rate * (fluid_at - velocity)
            force_ref[s, c : c + 1, :] = rate * (velocity - fluid_at)
        moved_ref[s, 3:8, :] = jnp.zeros((5, LANES), F32)
        force_ref[s, 3:4, :] = jnp.zeros((1, LANES), F32)


def scatter_kernel(parcel_ref, force_ref, out_ref, total_ref):
    rows = lax.broadcasted_iota(I32, (ROWS, LANES), 0)
    columns = lax.broadcasted_iota(I32, (LANES, LANES), 0)
    total_ref[...] = jnp.zeros_like(total_ref)
    for first in range(0, OWNERS, 4):
        left, right = [], []
        for s in range(first, first + 4):
            cells = parcel_ref[s, 8:16, :].astype(I32)
            high = lax.shift_right_logical(cells, 7)
            low = lax.bitwise_and(cells, 127)
            weights = LOADING * parcel_ref[s, 0:8, :]
            parts = []
            for c in range(3):
                value = weights * force_ref[s, c : c + 1, :]
                top = value.astype(BF16).astype(F32)
                parts.append(top)
                parts.append(value - top)
            for k in range(K):
                here = rows == wide(high[k : k + 1], ROWS)
                chosen = [jnp.where(here, wide(p[k : k + 1], ROWS), 0.0).astype(BF16) for p in parts]
                left.append(jnp.concatenate(chosen, axis=0))
                right.append((columns == wide(low[k : k + 1], LANES)).astype(F32).astype(BF16))
        total_ref[...] += lax.dot_general(
            jnp.concatenate(left, axis=1), jnp.concatenate(right, axis=1),
            (((1,), (1,)), ((), ())), preferred_element_type=F32,
        )
    for c in range(3):
        both = (
            total_ref[2 * c * ROWS : (2 * c + 1) * ROWS, :]
            + total_ref[(2 * c + 1) * ROWS : (2 * c + 2) * ROWS, :]
        )
        for r in range(ROWS):
            out_ref[c : c + 1, r * LANES : (r + 1) * LANES] = both[r : r + 1]


def return_kernel(place_ref, answer_ref, grad_ref, out_ref):
    for j in range(CHUNKS):
        cut = slice(j * LANES, (j + 1) * LANES)
        place = wide(place_ref[j : j + 1, :], 8)
        high = lax.shift_right_logical(place, 7)
        low = lax.bitwise_and(place, 127)
        pressure = jnp.zeros((8, LANES), F32)
        moved = jnp.zeros((8, LANES), F32)
        for o in range(OWNERS):
            here = high == o
            pressure = jnp.where(here, pick(answer_ref[o, 0:8, :], low), pressure)
            moved = jnp.where(here, pick(answer_ref[o, 8:16, :], low), moved)
        for c in range(3):
            gradient = jnp.sum(grad_ref[c, :, cut] * pressure, axis=0, keepdims=True)
            out_ref[c : c + 1, cut] = moved[c : c + 1] - gradient


def shape(*dims, dtype=F32):
    return jax.ShapeDtypeStruct(dims, dtype)


def pairs(count):
    first = [(i, i ^ 1) for i in range(count)]
    second = [(i, (i - 1) % count if i % 2 == 0 else (i + 1) % count) for i in range(count)]
    return first, second


def exchange(faces):
    dom_first, dom_second = pairs(lax.axis_size("dom"))
    group_first, group_second = pairs(lax.axis_size("group"))
    far = lax.ppermute(faces[1], "dom", dom_second)
    return (
        lax.ppermute(faces[0], "dom", dom_first),
        far,
        lax.ppermute(faces[2], "group", group_first),
        lax.ppermute(faces[3], "group", group_second),
    )


def call(kernel, outs, flops, scratch=(), grant=32, **kwargs):
    return pl.pallas_call(
        kernel,
        out_shape=outs,
        scratch_shapes=list(scratch),
        compiler_params=pltpu.CompilerParams(vmem_limit_bytes=grant * 1024 * 1024),
        cost_estimate=pl.CostEstimate(flops=flops, bytes_accessed=400000, transcendentals=0),
        **kwargs,
    )


def staged(kernel, operands, outs, flops, scratch=()):
    count = len(operands)

    def run(*refs):
        local, sems = refs[-1 - count : -1], refs[-1]
        copies = [
            pltpu.make_async_copy(refs[i], local[i], sems.at[i]) for i in range(count)
        ]
        for copy in copies:
            copy.start()
        for copy in copies:
            copy.wait()
        kernel(*local, *refs[count : -1 - count])

    scratch = (
        *scratch,
        *(pltpu.VMEM(x.shape, x.dtype) for x in operands),
        pltpu.SemaphoreType.DMA((count,)),
    )
    specs = [pl.BlockSpec(memory_space=pltpu.HBM)] * count
    return call(run, outs, flops, scratch, in_specs=specs)(*operands)


def per_device(
    pressure_old, source_term, diagonal, face_coeffs, neighbours, export_cells, fluid_velocity,
    parcel_velocity, drag_rate, parcel_owner, parcel_cells, interp_weights, grad_weights,
):
    pressure_old = pressure_old.reshape(ROWS, LANES)
    source_term = source_term.reshape(ROWS, LANES)
    diagonal = diagonal.reshape(ROWS, LANES)
    face = shape(FACE_ROWS, LANES)
    field = shape(ROWS, LANES)
    faces_buffer = pltpu.VMEM((4, FACE_ROWS, LANES), F32)
    halo = (pltpu.VMEM((4 * FACE_ROWS, LANES), F32), pltpu.VMEM((ROWS, LANES), F32))

    faces = staged(
        export_kernel, (pressure_old, export_cells), (face,) * 4, 10**6, (faces_buffer,)
    )
    got = exchange(faces)
    place, sent = staged(
        slot_kernel,
        (
            parcel_owner.reshape(CHUNKS, LANES), parcel_cells, interp_weights, parcel_velocity,
            drag_rate.reshape(CHUNKS, LANES),
        ),
        (shape(CHUNKS, LANES, dtype=I32), shape(OWNERS, SENT, CAP)), 10**8,
    )
    got, sent = lax.optimization_barrier((got, sent))
    parcels = lax.all_to_all(sent, "dom", split_axis=0, concat_axis=0, tiled=True)
    residual, direction, *faces = call(
        first_kernel, (field, field) + (face,) * 4, 10**8, halo + (faces_buffer,)
    )(pressure_old, *got, source_term, diagonal, face_coeffs, neighbours, export_cells)
    got = exchange(faces)
    moved, force = call(
        fluid_kernel, (shape(OWNERS, 8, CAP), shape(OWNERS, 4, CAP)), 10**9
    )(fluid_velocity, parcels)
    iterate, answer = call(second_kernel, (field, shape(OWNERS, 16, CAP)), 10**8, halo)(
        direction, *got, pressure_old, residual, diagonal, face_coeffs, neighbours, parcels, moved
    )
    returned = lax.all_to_all(answer, "dom", split_axis=0, concat_axis=0, tiled=True)
    momentum_source = call(
        scatter_kernel, shape(3, CELLS), 2 * 10**9, (pltpu.VMEM((6 * ROWS, LANES), F32),)
    )(parcels, force)
    parcel_new = call(return_kernel, shape(3, PARCELS), 10**6)(place, returned, grad_weights)
    return (iterate.reshape(CELLS), parcel_new, momentum_source)


def solution(mesh):
    whole = ("group", "dom")
    flat, rows = P(whole), P(None, whole)
    return jax.shard_map(
        per_device,
        mesh=mesh,
        in_specs=(
            flat, flat, flat, rows, rows, rows, rows, rows, flat, flat, rows, rows,
            P(None, None, whole),
        ),
        out_specs=(flat, rows, rows),
        check_vma=False,
    )
```

```python
import jax
import jax.numpy as jnp
from jax import lax
from jax.experimental import pallas as pl
from jax.experimental.pallas import tpu as pltpu
from jax.sharding import PartitionSpec as P

CENTRE = 7.0
HALF_WIDTH = 4.0
LOADING = 8.0
SIGMA = CENTRE / HALF_WIDTH
RHO_FIRST = 1.0 / SIGMA
RHO_NEXT = 1.0 / (2.0 * SIGMA - RHO_FIRST)

CELLS = 4096
LANES = 128
ROWS = CELLS // LANES
FACE = 1024
FACE_ROWS = FACE // LANES
NBR = 6
K = 8
PARCELS = 1024
CHUNKS = PARCELS // LANES
OWNERS = 32
CAP = 128
SENT = 24

F32 = jnp.float32
BF16 = jnp.bfloat16
I32 = jnp.int32


def pick(row, lanes):
    return jnp.take_along_axis(row, lanes, axis=1, mode="promise_in_bounds")


def wide(row, height):
    return jnp.broadcast_to(row, (height, LANES))


def look_up(tables, index):
    height = index.shape[0]
    high = lax.shift_right_logical(index, 7)
    low = lax.bitwise_and(index, 127)
    found = [jnp.zeros((height, LANES), F32) for _ in tables]
    for r in range(len(tables[0])):
        here = high == r
        for c, table in enumerate(tables):
            found[c] = jnp.where(here, pick(wide(table[r](), height), low), found[c])
    return found


def rows_of(ref, count):
    return [lambda r=r: ref[r : r + 1, :] for r in range(count)]


def is_even(axis):
    return lax.rem(lax.axis_index(axis), 2) == 0


def write_exports(field_ref, export_ref, face_ref, outs):
    for t in range(FACE_ROWS):
        index = export_ref[:, t * LANES : (t + 1) * LANES]
        (found,) = look_up([rows_of(field_ref, ROWS)], index)
        for d in range(4):
            face_ref[d, t : t + 1, :] = found[d : d + 1]
    for axis, d in (("dom", 0), ("group", 2)):
        even = is_even(axis)
        outs[d][...] = jnp.where(even, face_ref[d], face_ref[d + 1])
        outs[d + 1][...] = jnp.where(even, face_ref[d + 1], face_ref[d])


def export_kernel(ready, field_ref, export_ref, out0, out1, out2, out3, face_ref):
    ready(0)
    ready(1)
    write_exports(field_ref, export_ref, face_ref, (out0, out1, out2, out3))


def multiply(vector_ref, got_refs, diagonal_ref, coeff_ref, neighbour_ref, halo_ref, out_ref):
    group = lax.axis_index("group")
    last = lax.axis_size("group") - 1
    for axis, d in (("dom", 0), ("group", 2)):
        even = is_even(axis)
        below = jnp.where(even, got_refs[d + 1][...], got_refs[d][...])
        above = jnp.where(even, got_refs[d][...], got_refs[d + 1][...])
        if axis == "group":
            below = jnp.where(group > 0, below, 0.0)
            above = jnp.where(group < last, above, 0.0)
        halo_ref[d * FACE_ROWS : (d + 1) * FACE_ROWS, :] = below
        halo_ref[(d + 1) * FACE_ROWS : (d + 2) * FACE_ROWS, :] = above
    table = rows_of(vector_ref, ROWS) + rows_of(halo_ref, 4 * FACE_ROWS)
    for t in range(ROWS):
        cut, row = slice(t * LANES, (t + 1) * LANES), slice(t, t + 1)
        (found,) = look_up([table], neighbour_ref[:, cut])
        linked = jnp.sum(coeff_ref[:, cut] * found, axis=0, keepdims=True)
        out_ref[row, :] = diagonal_ref[row, :] * vector_ref[row, :] - linked


def first_kernel(
    pressure_ref, got0, got1, got2, got3, source_ref, diagonal_ref, coeff_ref, neighbour_ref,
    export_ref, residual_ref, direction_ref, out0, out1, out2, out3, halo_ref, product_ref, face_ref,
):
    multiply(
        pressure_ref, (got0, got1, got2, got3), diagonal_ref, coeff_ref, neighbour_ref,
        halo_ref, product_ref,
    )
    residual = source_ref[...] - product_ref[...]
    residual_ref[...] = residual
    direction_ref[...] = residual / CENTRE
    write_exports(direction_ref, export_ref, face_ref, (out0, out1, out2, out3))


def second_kernel(
    direction_ref, got0, got1, got2, got3, pressure_ref, residual_ref, diagonal_ref, coeff_ref,
    neighbour_ref, parcel_ref, moved_ref, out_ref, answer_ref, halo_ref, product_ref,
):
    multiply(
        direction_ref, (got0, got1, got2, got3), diagonal_ref, coeff_ref, neighbour_ref,
        halo_ref, product_ref,
    )
    direction = direction_ref[...]
    residual = residual_ref[...] - product_ref[...]
    iterate = pressure_ref[...] + direction
    direction = RHO_NEXT * RHO_FIRST * direction + (2.0 * RHO_NEXT / HALF_WIDTH) * residual
    out_ref[...] = iterate + direction
    table = rows_of(out_ref, ROWS)
    for s in range(OWNERS):
        (found,) = look_up([table], parcel_ref[s, 8:16, :].astype(I32))
        answer_ref[s, 0:8, :] = found
        answer_ref[s, 8:16, :] = moved_ref[s]


def slot_kernel(
    ready, owner_ref, cells_ref, weight_ref, velocity_ref, rate_ref, place_ref, sent_ref
):
    ready(0)
    owners = lax.broadcasted_iota(I32, (OWNERS, LANES), 0)
    lanes = lax.broadcasted_iota(I32, (OWNERS, LANES), 1)
    chosen = [owners == wide(owner_ref[j : j + 1, :], OWNERS) for j in range(CHUNKS)]
    stacked = jnp.concatenate([c.astype(F32).astype(BF16) for c in chosen], axis=0)
    row = lax.broadcasted_iota(I32, (LANES, 2 * LANES), 0)
    column = lax.broadcasted_iota(I32, (LANES, 2 * LANES), 1)
    before = ((row < column) | (column >= LANES)).astype(F32).astype(BF16)
    counts = jnp.dot(stacked, before, preferred_element_type=F32)
    carried = jnp.zeros((OWNERS, LANES), F32)
    ranks = []
    for j in range(CHUNKS):
        part = counts[j * OWNERS : (j + 1) * OWNERS]
        rank = jnp.where(chosen[j], part[:, :LANES] + carried, 0.0)
        ranks.append(jnp.sum(rank, axis=0, keepdims=True))
        carried = carried + part[:, LANES:]
        place_ref[j : j + 1, :] = owner_ref[j : j + 1, :] * CAP + ranks[j].astype(I32)
    slots = lax.broadcasted_iota(I32, (CAP, LANES), 0).astype(F32)
    at_rank = jnp.concatenate(
        [(slots == wide(ranks[j], CAP)).astype(F32).astype(BF16) for j in range(CHUNKS)], axis=1
    )
    lane_of = jnp.concatenate(
        [jnp.where(c, lanes.astype(F32), 0.0).astype(BF16) for c in chosen], axis=1
    )
    chunk_of = jnp.concatenate(
        [jnp.where(c, F32(j + 1), 0.0).astype(BF16) for j, c in enumerate(chosen)], axis=1
    )
    found = lax.dot_general(
        jnp.concatenate([lane_of, chunk_of], axis=0), at_rank, (((1,), (1,)), ((), ())),
        preferred_element_type=F32,
    ).astype(I32)
    for i in range(1, 5):
        ready(i)
    for o in range(OWNERS):
        low = wide(found[o : o + 1], 8)
        high = wide(found[OWNERS + o : OWNERS + o + 1], 8)
        here = [high == j + 1 for j in range(CHUNKS)]

        def place(ref, height=8):
            value = jnp.zeros((height, LANES), F32)
            for j in range(CHUNKS):
                part = ref[:, j * LANES : (j + 1) * LANES].astype(F32)
                value = jnp.where(here[j][:height], pick(part, low[:height]), value)
            return value

        sent_ref[o, 0:8, :] = place(weight_ref)
        sent_ref[o, 8:16, :] = place(cells_ref)
        sent_ref[o, 16:19, :] = place(velocity_ref, 3)
        value = jnp.zeros((8, LANES), F32)
        for j in range(CHUNKS):
            value = jnp.where(here[j], pick(wide(rate_ref[j : j + 1, :], 8), low), value)
        sent_ref[o, 19:24, :] = jnp.concatenate([value[:1], jnp.zeros((4, LANES), F32)], axis=0)


def fluid_kernel(fluid_ref, parcel_ref, moved_ref, force_ref):
    tables = [
        [lambda c=c, r=r: fluid_ref[c : c + 1, r * LANES : (r + 1) * LANES] for r in range(ROWS)]
        for c in range(3)
    ]
    for s in range(OWNERS):
        found = look_up(tables, parcel_ref[s, 8:16, :].astype(I32))
        weights = parcel_ref[s, 0:8, :]
        rate = parcel_ref[s, 19:20, :]
        for c in range(3):
            velocity = parcel_ref[s, 16 + c : 17 + c, :]
            fluid_at = jnp.sum(weights * found[c], axis=0, keepdims=True)
            moved_ref[s, c : c + 1, :] = velocity + rate * (fluid_at - velocity)
            force_ref[s, c : c + 1, :] = rate * (velocity - fluid_at)
        moved_ref[s, 3:8, :] = jnp.zeros((5, LANES), F32)
        force_ref[s, 3:4, :] = jnp.zeros((1, LANES), F32)


def scatter_kernel(parcel_ref, force_ref, out_ref, total_ref):
    rows = lax.broadcasted_iota(I32, (ROWS, LANES), 0)
    columns = lax.broadcasted_iota(I32, (LANES, LANES), 0)
    total_ref[...] = jnp.zeros_like(total_ref)
    for first in range(0, OWNERS, 4):
        left, right = [], []
        for s in range(first, first + 4):
            cells = parcel_ref[s, 8:16, :].astype(I32)
            high = lax.shift_right_logical(cells, 7)
            low = lax.bitwise_and(cells, 127)
            weights = LOADING * parcel_ref[s, 0:8, :]
            parts = []
            for c in range(3):
                value = weights * force_ref[s, c : c + 1, :]
                top = value.astype(BF16).astype(F32)
                parts.append(top)
                parts.append(value - top)
            for k in range(K):
                here = rows == wide(high[k : k + 1], ROWS)
                chosen = [jnp.where(here, wide(p[k : k + 1], ROWS), 0.0).astype(BF16) for p in parts]
                left.append(jnp.concatenate(chosen, axis=0))
                right.append((columns == wide(low[k : k + 1], LANES)).astype(F32).astype(BF16))
        total_ref[...] += lax.dot_general(
            jnp.concatenate(left, axis=1), jnp.concatenate(right, axis=1),
            (((1,), (1,)), ((), ())), preferred_element_type=F32,
        )
    for c in range(3):
        both = (
            total_ref[2 * c * ROWS : (2 * c + 1) * ROWS, :]
            + total_ref[(2 * c + 1) * ROWS : (2 * c + 2) * ROWS, :]
        )
        for r in range(ROWS):
            out_ref[c : c + 1, r * LANES : (r + 1) * LANES] = both[r : r + 1]


def return_kernel(place_ref, answer_ref, grad_ref, out_ref):
    for j in range(CHUNKS):
        cut = slice(j * LANES, (j + 1) * LANES)
        place = wide(place_ref[j : j + 1, :], 8)
        high = lax.shift_right_logical(place, 7)
        low = lax.bitwise_and(place, 127)
        pressure = jnp.zeros((8, LANES), F32)
        moved = jnp.zeros((8, LANES), F32)
        for o in range(OWNERS):
            here = high == o
            pressure = jnp.where(here, pick(answer_ref[o, 0:8, :], low), pressure)
            moved = jnp.where(here, pick(answer_ref[o, 8:16, :], low), moved)
        for c in range(3):
            gradient = jnp.sum(grad_ref[c, :, cut] * pressure, axis=0, keepdims=True)
            out_ref[c : c + 1, cut] = moved[c : c + 1] - gradient


def shape(*dims, dtype=F32):
    return jax.ShapeDtypeStruct(dims, dtype)


def exchange(faces):
    groups, count = lax.axis_size("group"), lax.axis_size("dom")
    near = [(m, m ^ 1) for m in range(count)]
    far = [(m, (m - 1 if m % 2 == 0 else m + 1) % count) for m in range(count)]
    over = [(g, g ^ 1) for g in range(groups)]
    under = []
    for g in range(groups):
        to = g - 1 if g % 2 == 0 else g + 1
        for m in range(count):
            inside = 0 <= to < groups
            under.append((g * count + m, to * count + m if inside else g * count + (m ^ 1)))
    return (
        lax.ppermute(faces[0], "dom", near),
        lax.ppermute(faces[1], "dom", far),
        lax.ppermute(faces[2], "group", over),
        lax.ppermute(faces[3], ("group", "dom"), under),
    )


def call(kernel, outs, flops, scratch=(), grant=32, **kwargs):
    return pl.pallas_call(
        kernel,
        out_shape=outs,
        scratch_shapes=list(scratch),
        compiler_params=pltpu.CompilerParams(vmem_limit_bytes=grant * 1024 * 1024),
        cost_estimate=pl.CostEstimate(flops=flops, bytes_accessed=400000, transcendentals=0),
        **kwargs,
    )


def staged(kernel, operands, outs, flops, scratch=()):
    count = len(operands)

    def run(*refs):
        local, sems = refs[-1 - count : -1], refs[-1]
        copies = [
            pltpu.make_async_copy(refs[i], local[i], sems.at[i]) for i in range(count)
        ]
        for copy in copies:
            copy.start()
        kernel(lambda i: copies[i].wait(), *local, *refs[count : -1 - count])

    scratch = (
        *scratch,
        *(pltpu.VMEM(x.shape, x.dtype) for x in operands),
        pltpu.SemaphoreType.DMA((count,)),
    )
    specs = [pl.BlockSpec(memory_space=pltpu.HBM)] * count
    operands = [pltpu.with_memory_space_constraint(x, pltpu.HBM) for x in operands]
    return call(run, outs, flops, scratch, in_specs=specs)(*operands)


def per_device(
    pressure_old, source_term, diagonal, face_coeffs, neighbours, export_cells, fluid_velocity,
    parcel_velocity, drag_rate, parcel_owner, parcel_cells, interp_weights, grad_weights,
):
    pressure_old = pressure_old.reshape(ROWS, LANES)
    source_term = source_term.reshape(ROWS, LANES)
    diagonal = diagonal.reshape(ROWS, LANES)
    face = shape(FACE_ROWS, LANES)
    field = shape(ROWS, LANES)
    faces_buffer = pltpu.VMEM((4, FACE_ROWS, LANES), F32)
    halo = (pltpu.VMEM((4 * FACE_ROWS, LANES), F32), pltpu.VMEM((ROWS, LANES), F32))

    faces = staged(
        export_kernel, (pressure_old, export_cells), (face,) * 4, 10**6, (faces_buffer,)
    )
    got = exchange(faces)
    place, sent = staged(
        slot_kernel,
        (
            parcel_owner.reshape(CHUNKS, LANES), parcel_cells, interp_weights, parcel_velocity,
            drag_rate.reshape(CHUNKS, LANES),
        ),
        (shape(CHUNKS, LANES, dtype=I32), shape(OWNERS, SENT, CAP)), 10**8,
    )
    got, sent = lax.optimization_barrier((got, sent))
    parcels = lax.all_to_all(sent, "dom", split_axis=0, concat_axis=0, tiled=True)
    residual, direction, *faces = call(
        first_kernel, (field, field) + (face,) * 4, 10**8, halo + (faces_buffer,)
    )(pressure_old, *got, source_term, diagonal, face_coeffs, neighbours, export_cells)
    got = exchange(faces)
    moved, force = call(
        fluid_kernel, (shape(OWNERS, 8, CAP), shape(OWNERS, 4, CAP)), 10**9
    )(fluid_velocity, parcels)
    iterate, answer = call(second_kernel, (field, shape(OWNERS, 16, CAP)), 10**8, halo)(
        direction, *got, pressure_old, residual, diagonal, face_coeffs, neighbours, parcels, moved
    )
    returned = lax.all_to_all(answer, "dom", split_axis=0, concat_axis=0, tiled=True)
    momentum_source = call(
        scatter_kernel, shape(3, CELLS), 2 * 10**9, (pltpu.VMEM((6 * ROWS, LANES), F32),)
    )(parcels, force)
    parcel_new = call(return_kernel, shape(3, PARCELS), 10**6)(place, returned, grad_weights)
    return (iterate.reshape(CELLS), parcel_new, momentum_source)


def solution(mesh):
    whole = ("group", "dom")
    flat, rows = P(whole), P(None, whole)
    return jax.shard_map(
        per_device,
        mesh=mesh,
        in_specs=(
            flat, flat, flat, rows, rows, rows, rows, rows, flat, flat, rows, rows,
            P(None, None, whole),
        ),
        out_specs=(flat, rows, rows),
        check_vma=False,
    )
```

```python
import jax
import jax.numpy as jnp
from jax import lax
from jax.experimental import pallas as pl
from jax.experimental.pallas import tpu as pltpu
from jax.sharding import PartitionSpec as P

CENTRE = 7.0
HALF_WIDTH = 4.0
LOADING = 8.0
SIGMA = CENTRE / HALF_WIDTH
RHO_FIRST = 1.0 / SIGMA
RHO_NEXT = 1.0 / (2.0 * SIGMA - RHO_FIRST)

CELLS = 4096
LANES = 128
ROWS = CELLS // LANES
FACE = 1024
FACE_ROWS = FACE // LANES
NBR = 6
K = 8
PARCELS = 1024
CHUNKS = PARCELS // LANES
OWNERS = 32
CAP = 128
SENT = 24
BACK = 16
PART = 8

F32 = jnp.float32
BF16 = jnp.bfloat16
I32 = jnp.int32


def pick(row, lanes):
    return jnp.take_along_axis(row, lanes, axis=1, mode="promise_in_bounds")


def wide(row, height):
    return jnp.broadcast_to(row, (height, LANES))


def look_up(tables, index):
    height = index.shape[0]
    high = lax.shift_right_logical(index, 7)
    low = lax.bitwise_and(index, 127)
    found = [jnp.zeros((height, LANES), F32) for _ in tables]
    for r in range(len(tables[0])):
        here = high == r
        for c, table in enumerate(tables):
            found[c] = jnp.where(here, pick(wide(table[r](), height), low), found[c])
    return found


def rows_of(ref, count):
    return [lambda r=r: ref[r : r + 1, :] for r in range(count)]


def is_even(axis):
    return lax.rem(lax.axis_index(axis), 2) == 0


def write_exports(field_ref, export_ref, face_ref, outs):
    for t in range(FACE_ROWS):
        index = export_ref[:, t * LANES : (t + 1) * LANES]
        (found,) = look_up([rows_of(field_ref, ROWS)], index)
        for d in range(4):
            face_ref[d, t : t + 1, :] = found[d : d + 1]
    for axis, d, first, second in (("dom", 0, outs[3], outs[0]), ("group", 2, outs[2], outs[1])):
        even = is_even(axis)
        first[...] = jnp.where(even, face_ref[d], face_ref[d + 1])
        second[...] = jnp.where(even, face_ref[d + 1], face_ref[d])


def export_kernel(*refs):
    (field_hbm, export_hbm), passed = refs[:2], refs[2:7]
    outs, passed_on = refs[7:11], refs[11:16]
    face_ref, field_ref, export_ref, sems = refs[16:]
    sources = (field_hbm, export_hbm) + passed
    targets = (field_ref, export_ref) + passed_on
    copies = [
        pltpu.make_async_copy(source, target, sems.at[i])
        for i, (source, target) in enumerate(zip(sources, targets))
    ]
    for copy in copies:
        copy.start()
    copies[0].wait()
    copies[1].wait()
    write_exports(field_ref, export_ref, face_ref, outs)
    for copy in copies[2:]:
        copy.wait()


def multiply(vector_ref, got_refs, diagonal_ref, coeff_ref, neighbour_ref, halo_ref, out_ref):
    group = lax.axis_index("group")
    last = lax.axis_size("group") - 1
    far, under, over, near = got_refs
    for axis, d, first, second in (("dom", 0, near, far), ("group", 2, over, under)):
        even = is_even(axis)
        below = jnp.where(even, second[...], first[...])
        above = jnp.where(even, first[...], second[...])
        if axis == "group":
            below = jnp.where(group > 0, below, 0.0)
            above = jnp.where(group < last, above, 0.0)
        halo_ref[d * FACE_ROWS : (d + 1) * FACE_ROWS, :] = below
        halo_ref[(d + 1) * FACE_ROWS : (d + 2) * FACE_ROWS, :] = above
    table = rows_of(vector_ref, ROWS) + rows_of(halo_ref, 4 * FACE_ROWS)
    for t in range(ROWS):
        cut, row = slice(t * LANES, (t + 1) * LANES), slice(t, t + 1)
        (found,) = look_up([table], neighbour_ref[:, cut])
        linked = jnp.sum(coeff_ref[:, cut] * found, axis=0, keepdims=True)
        out_ref[row, :] = diagonal_ref[row, :] * vector_ref[row, :] - linked


def first_kernel(
    pressure_ref, got0, got1, got2, got3, source_ref, diagonal_ref, coeff_ref, neighbour_ref,
    export_ref, residual_ref, direction_ref, out0, out1, out2, out3, halo_ref, product_ref, face_ref,
):
    multiply(
        pressure_ref, (got0, got1, got2, got3), diagonal_ref, coeff_ref, neighbour_ref,
        halo_ref, product_ref,
    )
    residual = source_ref[...] - product_ref[...]
    residual_ref[...] = residual
    direction_ref[...] = residual / CENTRE
    write_exports(direction_ref, export_ref, face_ref, (out0, out1, out2, out3))


def second_kernel(
    direction_ref, got0, got1, got2, got3, pressure_ref, residual_ref, diagonal_ref, coeff_ref,
    neighbour_ref, out_ref, again_ref, halo_ref, product_ref,
):
    multiply(
        direction_ref, (got0, got1, got2, got3), diagonal_ref, coeff_ref, neighbour_ref,
        halo_ref, product_ref,
    )
    direction = direction_ref[...]
    residual = residual_ref[...] - product_ref[...]
    iterate = pressure_ref[...] + direction
    direction = RHO_NEXT * RHO_FIRST * direction + (2.0 * RHO_NEXT / HALF_WIDTH) * residual
    out_ref[...] = iterate + direction
    again_ref[...] = iterate + direction


def send_out(local_ref, hbm_ref, sems, part):
    block = pl.ds(part * PART, PART)
    return pltpu.make_async_copy(local_ref.at[block], hbm_ref.at[block], sems.at[part])


def slot_kernel(
    owner_ref, cells_ref, weight_ref, velocity_ref, rate_ref, place_ref, sent_hbm, sent_ref,
    state_ref, sems,
):
    owners = lax.broadcasted_iota(I32, (OWNERS, LANES), 0)
    lanes = lax.broadcasted_iota(I32, (OWNERS, LANES), 1)
    chosen = [owners == wide(owner_ref[j : j + 1, :], OWNERS) for j in range(CHUNKS)]
    stacked = jnp.concatenate([c.astype(F32).astype(BF16) for c in chosen], axis=0)
    row = lax.broadcasted_iota(I32, (LANES, 2 * LANES), 0)
    column = lax.broadcasted_iota(I32, (LANES, 2 * LANES), 1)
    before = ((row < column) | (column >= LANES)).astype(F32).astype(BF16)
    counts = jnp.dot(stacked, before, preferred_element_type=F32)
    carried = jnp.zeros((OWNERS, LANES), F32)
    ranks = []
    for j in range(CHUNKS):
        part = counts[j * OWNERS : (j + 1) * OWNERS]
        rank = jnp.where(chosen[j], part[:, :LANES] + carried, 0.0)
        ranks.append(jnp.sum(rank, axis=0, keepdims=True))
        carried = carried + part[:, LANES:]
        place_ref[j : j + 1, :] = owner_ref[j : j + 1, :] * CAP + ranks[j].astype(I32)
    slots = lax.broadcasted_iota(I32, (CAP, LANES), 0).astype(F32)
    at_rank = jnp.concatenate(
        [(slots == wide(ranks[j], CAP)).astype(F32).astype(BF16) for j in range(CHUNKS)], axis=1
    )
    lane_of = jnp.concatenate(
        [jnp.where(c, lanes.astype(F32), 0.0).astype(BF16) for c in chosen], axis=1
    )
    chunk_of = jnp.concatenate(
        [jnp.where(c, F32(j + 1), 0.0).astype(BF16) for j, c in enumerate(chosen)], axis=1
    )
    found = lax.dot_general(
        jnp.concatenate([lane_of, chunk_of], axis=0), at_rank, (((1,), (1,)), ((), ())),
        preferred_element_type=F32,
    ).astype(I32)
    state_ref[0:3, :] = velocity_ref[...]
    for j in range(CHUNKS):
        state_ref[3:4, j * LANES : (j + 1) * LANES] = rate_ref[j : j + 1, :]
    state_ref[4:8, :] = jnp.zeros((4, PARCELS), F32)
    for o in range(OWNERS):
        low = wide(found[o : o + 1], 8)
        high = wide(found[OWNERS + o : OWNERS + o + 1], 8)
        here = [high == j + 1 for j in range(CHUNKS)]

        def place(ref):
            value = jnp.zeros((8, LANES), F32)
            for j in range(CHUNKS):
                part = ref[:, j * LANES : (j + 1) * LANES].astype(F32)
                value = jnp.where(here[j], pick(part, low), value)
            return value

        sent_ref[o, 0:8, :] = place(weight_ref)
        sent_ref[o, 8:16, :] = place(cells_ref)
        sent_ref[o, 16:24, :] = place(state_ref)
        if o % PART == PART - 1:
            send_out(sent_ref, sent_hbm, sems, o // PART).start()
    for part in range(OWNERS // PART):
        send_out(sent_ref, sent_hbm, sems, part).wait()


def parcel_kernel(
    fluid_ref, pressure_ref, parcel_ref, answer_hbm, force_ref, answer_ref, sems
):
    tables = [
        [lambda c=c, r=r: fluid_ref[c : c + 1, r * LANES : (r + 1) * LANES] for r in range(ROWS)]
        for c in range(3)
    ]
    tables.append(rows_of(pressure_ref, ROWS))
    for s in range(OWNERS):
        *found, pressure = look_up(tables, parcel_ref[s, 8:16, :].astype(I32))
        answer_ref[s, 0:8, :] = pressure
        weights = parcel_ref[s, 0:8, :]
        rate = parcel_ref[s, 19:20, :]
        for c in range(3):
            velocity = parcel_ref[s, 16 + c : 17 + c, :]
            fluid_at = jnp.sum(weights * found[c], axis=0, keepdims=True)
            answer_ref[s, 8 + c : 9 + c, :] = velocity + rate * (fluid_at - velocity)
            force_ref[s, c : c + 1, :] = rate * (velocity - fluid_at)
        answer_ref[s, 11:16, :] = jnp.zeros((5, LANES), F32)
        force_ref[s, 3:4, :] = jnp.zeros((1, LANES), F32)
        if s % PART == PART - 1:
            send_out(answer_ref, answer_hbm, sems, s // PART).start()
    for part in range(OWNERS // PART):
        send_out(answer_ref, answer_hbm, sems, part).wait()


def scatter_kernel(parcel_ref, force_ref, out_ref, total_ref):
    rows = lax.broadcasted_iota(I32, (ROWS, LANES), 0)
    columns = lax.broadcasted_iota(I32, (LANES, LANES), 0)
    total_ref[...] = jnp.zeros_like(total_ref)
    for first in range(0, OWNERS, 4):
        left, right = [], []
        for s in range(first, first + 4):
            cells = parcel_ref[s, 8:16, :].astype(I32)
            high = lax.shift_right_logical(cells, 7)
            low = lax.bitwise_and(cells, 127)
            weights = LOADING * parcel_ref[s, 0:8, :]
            parts = []
            for c in range(3):
                value = weights * force_ref[s, c : c + 1, :]
                top = value.astype(BF16).astype(F32)
                parts.append(top)
                parts.append(value - top)
            for k in range(K):
                here = rows == wide(high[k : k + 1], ROWS)
                chosen = [jnp.where(here, wide(p[k : k + 1], ROWS), 0.0).astype(BF16) for p in parts]
                left.append(jnp.concatenate(chosen, axis=0))
                right.append((columns == wide(low[k : k + 1], LANES)).astype(F32).astype(BF16))
        total_ref[...] += lax.dot_general(
            jnp.concatenate(left, axis=1), jnp.concatenate(right, axis=1),
            (((1,), (1,)), ((), ())), preferred_element_type=F32,
        )
    for c in range(3):
        both = (
            total_ref[2 * c * ROWS : (2 * c + 1) * ROWS, :]
            + total_ref[(2 * c + 1) * ROWS : (2 * c + 2) * ROWS, :]
        )
        for r in range(ROWS):
            out_ref[c : c + 1, r * LANES : (r + 1) * LANES] = both[r : r + 1]


def return_kernel(place_ref, answer_ref, grad_ref, out_ref):
    for j in range(CHUNKS):
        cut = slice(j * LANES, (j + 1) * LANES)
        place = wide(place_ref[j : j + 1, :], 8)
        high = lax.shift_right_logical(place, 7)
        low = lax.bitwise_and(place, 127)
        pressure = jnp.zeros((8, LANES), F32)
        moved = jnp.zeros((8, LANES), F32)
        for o in range(OWNERS):
            here = high == o
            pressure = jnp.where(here, pick(answer_ref[o, 0:8, :], low), pressure)
            moved = jnp.where(here, pick(answer_ref[o, 8:16, :], low), moved)
        for c in range(3):
            gradient = jnp.sum(grad_ref[c, :, cut] * pressure, axis=0, keepdims=True)
            out_ref[c : c + 1, cut] = moved[c : c + 1] - gradient


def shape(*dims, dtype=F32):
    return jax.ShapeDtypeStruct(dims, dtype)


def exchange(faces):
    groups, count = lax.axis_size("group"), lax.axis_size("dom")
    near = [(m, m ^ 1) for m in range(count)]
    far = [(m, (m - 1 if m % 2 == 0 else m + 1) % count) for m in range(count)]
    over = [(g, g ^ 1) for g in range(groups)]
    under = []
    for g in range(groups):
        to = g - 1 if g % 2 == 0 else g + 1
        for m in range(count):
            inside = 0 <= to < groups
            under.append((g * count + m, to * count + m if inside else g * count + (m ^ 1)))
    return (
        lax.ppermute(faces[0], "dom", far),
        lax.ppermute(faces[1], ("group", "dom"), under),
        lax.ppermute(faces[2], "group", over),
        lax.ppermute(faces[3], "dom", near),
    )


def call(kernel, outs, flops, scratch=(), grant=32, **kwargs):
    return pl.pallas_call(
        kernel,
        out_shape=outs,
        scratch_shapes=list(scratch),
        compiler_params=pltpu.CompilerParams(vmem_limit_bytes=grant * 1024 * 1024),
        cost_estimate=pl.CostEstimate(flops=flops, bytes_accessed=400000, transcendentals=0),
        **kwargs,
    )


def per_device(
    pressure_old, source_term, diagonal, face_coeffs, neighbours, export_cells, fluid_velocity,
    parcel_velocity, drag_rate, parcel_owner, parcel_cells, interp_weights, grad_weights,
):
    pressure_old = pressure_old.reshape(ROWS, LANES)
    source_term = source_term.reshape(ROWS, LANES)
    diagonal = diagonal.reshape(ROWS, LANES)
    face = shape(FACE_ROWS, LANES)
    field = shape(ROWS, LANES)
    faces_buffer = pltpu.VMEM((4, FACE_ROWS, LANES), F32)
    halo = (pltpu.VMEM((4 * FACE_ROWS, LANES), F32), pltpu.VMEM((ROWS, LANES), F32))

    kept = [
        pltpu.with_memory_space_constraint(x, pltpu.HBM)
        for x in (
            pressure_old, export_cells, parcel_owner.reshape(CHUNKS, LANES), parcel_cells,
            interp_weights, parcel_velocity, drag_rate.reshape(CHUNKS, LANES),
        )
    ]
    outs = call(
        export_kernel,
        (face,) * 4 + tuple(shape(*x.shape, dtype=x.dtype) for x in kept[2:]),
        10**6,
        (
            faces_buffer, pltpu.VMEM((ROWS, LANES), F32), pltpu.VMEM((4, FACE), I32),
            pltpu.SemaphoreType.DMA((len(kept),)),
        ),
        in_specs=[pl.BlockSpec(memory_space=pltpu.HBM)] * len(kept),
    )(*kept)
    got = exchange(outs[:4])
    whole = pl.BlockSpec(memory_space=pltpu.VMEM)
    outside = pl.BlockSpec(memory_space=pl.ANY)
    parts = pltpu.SemaphoreType.DMA((OWNERS // PART,))
    place, sent = call(
        slot_kernel, (shape(CHUNKS, LANES, dtype=I32), shape(OWNERS, SENT, CAP)), 10**8,
        (pltpu.VMEM((OWNERS, SENT, CAP), F32), pltpu.VMEM((8, PARCELS), F32), parts),
        out_specs=(whole, outside),
    )(*outs[4:])
    got, sent = lax.optimization_barrier((got, sent))
    parcels = lax.all_to_all(sent, "dom", split_axis=0, concat_axis=0, tiled=True)
    residual, direction, *faces = call(
        first_kernel, (field, field) + (face,) * 4, 10**8, halo + (faces_buffer,)
    )(pressure_old, *got, source_term, diagonal, face_coeffs, neighbours, export_cells)
    got = exchange(faces)
    iterate, table = call(second_kernel, (field, field), 10**8, halo)(
        direction, *got, pressure_old, residual, diagonal, face_coeffs, neighbours
    )
    answer, force = call(
        parcel_kernel, (shape(OWNERS, BACK, CAP), shape(OWNERS, 4, CAP)), 10**9,
        (pltpu.VMEM((OWNERS, BACK, CAP), F32), parts),
        out_specs=(outside, whole),
    )(fluid_velocity, table, parcels)
    returned = lax.all_to_all(answer, "dom", split_axis=0, concat_axis=0, tiled=True)
    momentum_source = call(
        scatter_kernel, shape(3, CELLS), 2 * 10**9, (pltpu.VMEM((6 * ROWS, LANES), F32),)
    )(parcels, force)
    parcel_new = call(return_kernel, shape(3, PARCELS), 10**6)(place, returned, grad_weights)
    return (iterate.reshape(CELLS), parcel_new, momentum_source)


def solution(mesh):
    whole = ("group", "dom")
    flat, rows = P(whole), P(None, whole)
    return jax.shard_map(
        per_device,
        mesh=mesh,
        in_specs=(
            flat, flat, flat, rows, rows, rows, rows, rows, flat, flat, rows, rows,
            P(None, None, whole),
        ),
        out_specs=(flat, rows, rows),
        check_vma=False,
    )
```

```python
import jax
import jax.numpy as jnp
from jax import lax
from jax.experimental import pallas as pl
from jax.experimental.pallas import tpu as pltpu
from jax.sharding import PartitionSpec as P

CENTRE = 7.0
HALF_WIDTH = 4.0
LOADING = 8.0
SIGMA = CENTRE / HALF_WIDTH
RHO_FIRST = 1.0 / SIGMA
RHO_NEXT = 1.0 / (2.0 * SIGMA - RHO_FIRST)

CELLS = 4096
LANES = 128
ROWS = CELLS // LANES
FACE = 1024
FACE_ROWS = FACE // LANES
NBR = 6
K = 8
PARCELS = 1024
CHUNKS = PARCELS // LANES
OWNERS = 32
CAP = 128
SENT = 24
BACK = 16
PART = 8

F32 = jnp.float32
BF16 = jnp.bfloat16
I32 = jnp.int32


def pick(row, lanes):
    return jnp.take_along_axis(row, lanes, axis=1, mode="promise_in_bounds")


def wide(row, height):
    return jnp.broadcast_to(row, (height, LANES))


def look_up(tables, index):
    height = index.shape[0]
    high = lax.shift_right_logical(index, 7)
    low = lax.bitwise_and(index, 127)
    found = [jnp.zeros((height, LANES), F32) for _ in tables]
    for r in range(len(tables[0])):
        here = high == r
        for c, table in enumerate(tables):
            found[c] = jnp.where(here, pick(wide(table[r](), height), low), found[c])
    return found


def rows_of(ref, count):
    return [lambda r=r: ref[r : r + 1, :] for r in range(count)]


def is_even(axis):
    return lax.rem(lax.axis_index(axis), 2) == 0


def write_exports(field_ref, export_ref, face_ref, outs):
    for t in range(FACE_ROWS):
        index = export_ref[:, t * LANES : (t + 1) * LANES]
        (found,) = look_up([rows_of(field_ref, ROWS)], index)
        for d in range(4):
            face_ref[d, t : t + 1, :] = found[d : d + 1]
    for axis, d, first, second in (("dom", 0, outs[3], outs[0]), ("group", 2, outs[2], outs[1])):
        even = is_even(axis)
        first[...] = jnp.where(even, face_ref[d], face_ref[d + 1])
        second[...] = jnp.where(even, face_ref[d + 1], face_ref[d])


def export_kernel(*refs):
    (field_hbm, export_hbm), passed = refs[:2], refs[2:7]
    outs, passed_on = refs[7:11], refs[11:16]
    face_ref, field_ref, export_ref, sems = refs[16:]
    sources = (field_hbm, export_hbm) + passed
    targets = (field_ref, export_ref) + passed_on
    copies = [
        pltpu.make_async_copy(source, target, sems.at[i])
        for i, (source, target) in enumerate(zip(sources, targets))
    ]
    for copy in copies:
        copy.start()
    copies[0].wait()
    copies[1].wait()
    write_exports(field_ref, export_ref, face_ref, outs)
    for copy in copies[2:]:
        copy.wait()


def own_kernel(vector_ref, diagonal_ref, coeff_ref, neighbour_ref, out_ref):
    table = rows_of(vector_ref, ROWS)
    for t in range(ROWS):
        cut, row = slice(t * LANES, (t + 1) * LANES), slice(t, t + 1)
        (found,) = look_up([table], neighbour_ref[:, cut])
        linked = jnp.sum(coeff_ref[:, cut] * found, axis=0, keepdims=True)
        out_ref[row, :] = diagonal_ref[row, :] * vector_ref[row, :] - linked


def multiply(own_ref, got_refs, coeff_ref, neighbour_ref, halo_ref, out_ref):
    group = lax.axis_index("group")
    last = lax.axis_size("group") - 1
    far, under, over, near = got_refs
    for axis, d, first, second in (("dom", 0, near, far), ("group", 2, over, under)):
        even = is_even(axis)
        below = jnp.where(even, second[...], first[...])
        above = jnp.where(even, first[...], second[...])
        if axis == "group":
            below = jnp.where(group > 0, below, 0.0)
            above = jnp.where(group < last, above, 0.0)
        halo_ref[d * FACE_ROWS : (d + 1) * FACE_ROWS, :] = below
        halo_ref[(d + 1) * FACE_ROWS : (d + 2) * FACE_ROWS, :] = above
    table = rows_of(halo_ref, 4 * FACE_ROWS)
    for t in range(ROWS):
        cut, row = slice(t * LANES, (t + 1) * LANES), slice(t, t + 1)
        (found,) = look_up([table], neighbour_ref[:, cut] - CELLS)
        linked = jnp.sum(coeff_ref[:, cut] * found, axis=0, keepdims=True)
        out_ref[row, :] = own_ref[row, :] - linked


def first_kernel(
    pressure_ref, got0, got1, got2, got3, source_ref, diagonal_ref, coeff_ref, neighbour_ref,
    export_ref, residual_ref, direction_ref, out0, out1, out2, out3, halo_ref, product_ref,
    own_ref, face_ref,
):
    own_kernel(pressure_ref, diagonal_ref, coeff_ref, neighbour_ref, own_ref)
    multiply(own_ref, (got0, got1, got2, got3), coeff_ref, neighbour_ref, halo_ref, product_ref)
    residual = source_ref[...] - product_ref[...]
    residual_ref[...] = residual
    direction_ref[...] = residual / CENTRE
    write_exports(direction_ref, export_ref, face_ref, (out0, out1, out2, out3))


def second_kernel(
    own_ref, got0, got1, got2, got3, direction_ref, pressure_ref, residual_ref, coeff_ref,
    neighbour_ref, parcel_ref, moved_ref, out_ref, answer_hbm, halo_ref, product_ref, answer_ref,
    sems,
):
    multiply(own_ref, (got0, got1, got2, got3), coeff_ref, neighbour_ref, halo_ref, product_ref)
    direction = direction_ref[...]
    residual = residual_ref[...] - product_ref[...]
    iterate = pressure_ref[...] + direction
    direction = RHO_NEXT * RHO_FIRST * direction + (2.0 * RHO_NEXT / HALF_WIDTH) * residual
    out_ref[...] = iterate + direction
    table = rows_of(out_ref, ROWS)
    for s in range(OWNERS):
        (found,) = look_up([table], parcel_ref[s, 8:16, :].astype(I32))
        answer_ref[s, 0:8, :] = found
        answer_ref[s, 8:16, :] = moved_ref[s]
        if s % PART == PART - 1:
            send_out(answer_ref, answer_hbm, sems, s // PART).start()
    for part in range(OWNERS // PART):
        send_out(answer_ref, answer_hbm, sems, part).wait()


def send_out(local_ref, hbm_ref, sems, part):
    block = pl.ds(part * PART, PART)
    return pltpu.make_async_copy(local_ref.at[block], hbm_ref.at[block], sems.at[part])


def slot_kernel(
    owner_ref, cells_ref, weight_ref, velocity_ref, rate_ref, place_ref, sent_hbm, sent_ref,
    state_ref, sems,
):
    owners = lax.broadcasted_iota(I32, (OWNERS, LANES), 0)
    lanes = lax.broadcasted_iota(I32, (OWNERS, LANES), 1)
    chosen = [owners == wide(owner_ref[j : j + 1, :], OWNERS) for j in range(CHUNKS)]
    stacked = jnp.concatenate([c.astype(F32).astype(BF16) for c in chosen], axis=0)
    row = lax.broadcasted_iota(I32, (LANES, 2 * LANES), 0)
    column = lax.broadcasted_iota(I32, (LANES, 2 * LANES), 1)
    before = ((row < column) | (column >= LANES)).astype(F32).astype(BF16)
    counts = jnp.dot(stacked, before, preferred_element_type=F32)
    carried = jnp.zeros((OWNERS, LANES), F32)
    ranks = []
    for j in range(CHUNKS):
        part = counts[j * OWNERS : (j + 1) * OWNERS]
        rank = jnp.where(chosen[j], part[:, :LANES] + carried, 0.0)
        ranks.append(jnp.sum(rank, axis=0, keepdims=True))
        carried = carried + part[:, LANES:]
        place_ref[j : j + 1, :] = owner_ref[j : j + 1, :] * CAP + ranks[j].astype(I32)
    slots = lax.broadcasted_iota(I32, (CAP, LANES), 0).astype(F32)
    at_rank = jnp.concatenate(
        [(slots == wide(ranks[j], CAP)).astype(F32).astype(BF16) for j in range(CHUNKS)], axis=1
    )
    lane_of = jnp.concatenate(
        [jnp.where(c, lanes.astype(F32), 0.0).astype(BF16) for c in chosen], axis=1
    )
    chunk_of = jnp.concatenate(
        [jnp.where(c, F32(j + 1), 0.0).astype(BF16) for j, c in enumerate(chosen)], axis=1
    )
    found = lax.dot_general(
        jnp.concatenate([lane_of, chunk_of], axis=0), at_rank, (((1,), (1,)), ((), ())),
        preferred_element_type=F32,
    ).astype(I32)
    state_ref[0:3, :] = velocity_ref[...]
    for j in range(CHUNKS):
        state_ref[3:4, j * LANES : (j + 1) * LANES] = rate_ref[j : j + 1, :]
    state_ref[4:8, :] = jnp.zeros((4, PARCELS), F32)
    for o in range(OWNERS):
        low = wide(found[o : o + 1], 8)
        high = wide(found[OWNERS + o : OWNERS + o + 1], 8)
        here = [high == j + 1 for j in range(CHUNKS)]

        def place(ref):
            value = jnp.zeros((8, LANES), F32)
            for j in range(CHUNKS):
                part = ref[:, j * LANES : (j + 1) * LANES].astype(F32)
                value = jnp.where(here[j], pick(part, low), value)
            return value

        sent_ref[o, 0:8, :] = place(weight_ref)
        sent_ref[o, 8:16, :] = place(cells_ref)
        sent_ref[o, 16:24, :] = place(state_ref)
        if o % PART == PART - 1:
            send_out(sent_ref, sent_hbm, sems, o // PART).start()
    for part in range(OWNERS // PART):
        send_out(sent_ref, sent_hbm, sems, part).wait()


def fluid_kernel(fluid_ref, parcel_ref, moved_ref, force_ref):
    tables = [
        [lambda c=c, r=r: fluid_ref[c : c + 1, r * LANES : (r + 1) * LANES] for r in range(ROWS)]
        for c in range(3)
    ]
    for s in range(OWNERS):
        found = look_up(tables, parcel_ref[s, 8:16, :].astype(I32))
        weights = parcel_ref[s, 0:8, :]
        rate = parcel_ref[s, 19:20, :]
        for c in range(3):
            velocity = parcel_ref[s, 16 + c : 17 + c, :]
            fluid_at = jnp.sum(weights * found[c], axis=0, keepdims=True)
            moved_ref[s, c : c + 1, :] = velocity + rate * (fluid_at - velocity)
            force_ref[s, c : c + 1, :] = rate * (velocity - fluid_at)
        moved_ref[s, 3:8, :] = jnp.zeros((5, LANES), F32)
        force_ref[s, 3:4, :] = jnp.zeros((1, LANES), F32)


def scatter_kernel(parcel_ref, force_ref, out_ref, total_ref):
    rows = lax.broadcasted_iota(I32, (ROWS, LANES), 0)
    columns = lax.broadcasted_iota(I32, (LANES, LANES), 0)
    total_ref[...] = jnp.zeros_like(total_ref)
    for first in range(0, OWNERS, 4):
        left, right = [], []
        for s in range(first, first + 4):
            cells = parcel_ref[s, 8:16, :].astype(I32)
            high = lax.shift_right_logical(cells, 7)
            low = lax.bitwise_and(cells, 127)
            weights = LOADING * parcel_ref[s, 0:8, :]
            parts = []
            for c in range(3):
                value = weights * force_ref[s, c : c + 1, :]
                top = value.astype(BF16).astype(F32)
                parts.append(top)
                parts.append(value - top)
            for k in range(K):
                here = rows == wide(high[k : k + 1], ROWS)
                chosen = [jnp.where(here, wide(p[k : k + 1], ROWS), 0.0).astype(BF16) for p in parts]
                left.append(jnp.concatenate(chosen, axis=0))
                right.append((columns == wide(low[k : k + 1], LANES)).astype(F32).astype(BF16))
        total_ref[...] += lax.dot_general(
            jnp.concatenate(left, axis=1), jnp.concatenate(right, axis=1),
            (((1,), (1,)), ((), ())), preferred_element_type=F32,
        )
    for c in range(3):
        both = (
            total_ref[2 * c * ROWS : (2 * c + 1) * ROWS, :]
            + total_ref[(2 * c + 1) * ROWS : (2 * c + 2) * ROWS, :]
        )
        for r in range(ROWS):
            out_ref[c : c + 1, r * LANES : (r + 1) * LANES] = both[r : r + 1]


def return_kernel(place_ref, answer_ref, grad_ref, out_ref):
    for j in range(CHUNKS):
        cut = slice(j * LANES, (j + 1) * LANES)
        place = wide(place_ref[j : j + 1, :], 8)
        high = lax.shift_right_logical(place, 7)
        low = lax.bitwise_and(place, 127)
        pressure = jnp.zeros((8, LANES), F32)
        moved = jnp.zeros((8, LANES), F32)
        for o in range(OWNERS):
            here = high == o
            pressure = jnp.where(here, pick(answer_ref[o, 0:8, :], low), pressure)
            moved = jnp.where(here, pick(answer_ref[o, 8:16, :], low), moved)
        for c in range(3):
            gradient = jnp.sum(grad_ref[c, :, cut] * pressure, axis=0, keepdims=True)
            out_ref[c : c + 1, cut] = moved[c : c + 1] - gradient


def shape(*dims, dtype=F32):
    return jax.ShapeDtypeStruct(dims, dtype)


def exchange(faces):
    groups, count = lax.axis_size("group"), lax.axis_size("dom")
    near = [(m, m ^ 1) for m in range(count)]
    far = [(m, (m - 1 if m % 2 == 0 else m + 1) % count) for m in range(count)]
    over = [(g, g ^ 1) for g in range(groups)]
    under = []
    for g in range(groups):
        to = g - 1 if g % 2 == 0 else g + 1
        for m in range(count):
            inside = 0 <= to < groups
            under.append((g * count + m, to * count + m if inside else g * count + (m ^ 1)))
    return (
        lax.ppermute(faces[0], "dom", far),
        lax.ppermute(faces[1], ("group", "dom"), under),
        lax.ppermute(faces[2], "group", over),
        lax.ppermute(faces[3], "dom", near),
    )


def call(kernel, outs, flops, scratch=(), grant=32, **kwargs):
    return pl.pallas_call(
        kernel,
        out_shape=outs,
        scratch_shapes=list(scratch),
        compiler_params=pltpu.CompilerParams(vmem_limit_bytes=grant * 1024 * 1024),
        cost_estimate=pl.CostEstimate(flops=flops, bytes_accessed=400000, transcendentals=0),
        **kwargs,
    )


def per_device(
    pressure_old, source_term, diagonal, face_coeffs, neighbours, export_cells, fluid_velocity,
    parcel_velocity, drag_rate, parcel_owner, parcel_cells, interp_weights, grad_weights,
):
    pressure_old = pressure_old.reshape(ROWS, LANES)
    source_term = source_term.reshape(ROWS, LANES)
    diagonal = diagonal.reshape(ROWS, LANES)
    face = shape(FACE_ROWS, LANES)
    field = shape(ROWS, LANES)
    faces_buffer = pltpu.VMEM((4, FACE_ROWS, LANES), F32)
    halo = (pltpu.VMEM((4 * FACE_ROWS, LANES), F32), pltpu.VMEM((ROWS, LANES), F32))

    kept = [
        pltpu.with_memory_space_constraint(x, pltpu.HBM)
        for x in (
            pressure_old, export_cells, parcel_owner.reshape(CHUNKS, LANES), parcel_cells,
            interp_weights, parcel_velocity, drag_rate.reshape(CHUNKS, LANES),
        )
    ]
    outs = call(
        export_kernel,
        (face,) * 4 + tuple(shape(*x.shape, dtype=x.dtype) for x in kept[2:]),
        10**6,
        (
            faces_buffer, pltpu.VMEM((ROWS, LANES), F32), pltpu.VMEM((4, FACE), I32),
            pltpu.SemaphoreType.DMA((len(kept),)),
        ),
        in_specs=[pl.BlockSpec(memory_space=pltpu.HBM)] * len(kept),
    )(*kept)
    got = exchange(outs[:4])
    everything = pl.BlockSpec(memory_space=pltpu.VMEM)
    outside = pl.BlockSpec(memory_space=pl.ANY)
    parts = pltpu.SemaphoreType.DMA((OWNERS // PART,))
    place, sent = call(
        slot_kernel, (shape(CHUNKS, LANES, dtype=I32), shape(OWNERS, SENT, CAP)), 10**8,
        (pltpu.VMEM((OWNERS, SENT, CAP), F32), pltpu.VMEM((8, PARCELS), F32), parts),
        out_specs=(everything, outside),
    )(*outs[4:])
    got, sent = lax.optimization_barrier((got, sent))
    parcels = lax.all_to_all(sent, "dom", split_axis=0, concat_axis=0, tiled=True)
    residual, direction, *faces = call(
        first_kernel, (field, field) + (face,) * 4, 10**8,
        halo + (pltpu.VMEM((ROWS, LANES), F32), faces_buffer),
    )(pressure_old, *got, source_term, diagonal, face_coeffs, neighbours, export_cells)
    got = exchange(faces)
    own = call(own_kernel, field, 10**7)(direction, diagonal, face_coeffs, neighbours)
    moved, force = call(
        fluid_kernel, (shape(OWNERS, 8, CAP), shape(OWNERS, 4, CAP)), 10**9
    )(fluid_velocity, parcels)
    iterate, answer = call(
        second_kernel, (field, shape(OWNERS, BACK, CAP)), 10**8,
        halo + (pltpu.VMEM((OWNERS, BACK, CAP), F32), parts),
        out_specs=(everything, outside),
    )(
        own, *got, direction, pressure_old, residual, face_coeffs, neighbours, parcels, moved
    )
    returned = lax.all_to_all(answer, "dom", split_axis=0, concat_axis=0, tiled=True)
    momentum_source = call(
        scatter_kernel, shape(3, CELLS), 2 * 10**9, (pltpu.VMEM((6 * ROWS, LANES), F32),)
    )(parcels, force)
    parcel_new = call(return_kernel, shape(3, PARCELS), 10**6)(place, returned, grad_weights)
    return (iterate.reshape(CELLS), parcel_new, momentum_source)


def solution(mesh):
    whole = ("group", "dom")
    flat, rows = P(whole), P(None, whole)
    return jax.shard_map(
        per_device,
        mesh=mesh,
        in_specs=(
            flat, flat, flat, rows, rows, rows, rows, rows, flat, flat, rows, rows,
            P(None, None, whole),
        ),
        out_specs=(flat, rows, rows),
        check_vma=False,
    )
```

```python
import jax
import jax.numpy as jnp
from jax import lax
from jax.experimental import pallas as pl
from jax.experimental.pallas import tpu as pltpu
from jax.sharding import PartitionSpec as P

CENTRE = 7.0
HALF_WIDTH = 4.0
LOADING = 8.0
SIGMA = CENTRE / HALF_WIDTH
RHO_FIRST = 1.0 / SIGMA
RHO_NEXT = 1.0 / (2.0 * SIGMA - RHO_FIRST)

CELLS = 4096
LANES = 128
ROWS = CELLS // LANES
FACE = 1024
FACE_ROWS = FACE // LANES
NBR = 6
K = 8
PARCELS = 1024
CHUNKS = PARCELS // LANES
OWNERS = 32
CAP = 128
SENT = 24
BACK = 16
PART = 8

F32 = jnp.float32
BF16 = jnp.bfloat16
I32 = jnp.int32


def pick(row, lanes):
    return jnp.take_along_axis(row, lanes, axis=1, mode="promise_in_bounds")


def wide(row, height):
    return jnp.broadcast_to(row, (height, LANES))


def look_up(tables, index):
    height = index.shape[0]
    high = lax.shift_right_logical(index, 7)
    low = lax.bitwise_and(index, 127)
    found = [jnp.zeros((height, LANES), F32) for _ in tables]
    for r in range(len(tables[0])):
        here = high == r
        for c, table in enumerate(tables):
            found[c] = jnp.where(here, pick(wide(table[r](), height), low), found[c])
    return found


def rows_of(ref, count):
    return [lambda r=r: ref[r : r + 1, :] for r in range(count)]


def is_even(axis):
    return lax.rem(lax.axis_index(axis), 2) == 0


def write_exports(field_ref, export_ref, face_ref, outs):
    for t in range(FACE_ROWS):
        index = export_ref[:, t * LANES : (t + 1) * LANES]
        (found,) = look_up([rows_of(field_ref, ROWS)], index)
        for d in range(4):
            face_ref[d, t : t + 1, :] = found[d : d + 1]
    for axis, d, first, second in (("dom", 0, outs[3], outs[0]), ("group", 2, outs[1], outs[2])):
        even = is_even(axis)
        first[...] = jnp.where(even, face_ref[d], face_ref[d + 1])
        second[...] = jnp.where(even, face_ref[d + 1], face_ref[d])


def export_kernel(*refs):
    (field_hbm, export_hbm), passed = refs[:2], refs[2:7]
    outs, passed_on = refs[7:11], refs[11:16]
    face_ref, field_ref, export_ref, sems = refs[16:]
    sources = (field_hbm, export_hbm) + passed
    targets = (field_ref, export_ref) + passed_on
    copies = [
        pltpu.make_async_copy(source, target, sems.at[i])
        for i, (source, target) in enumerate(zip(sources, targets))
    ]
    for copy in copies:
        copy.start()
    copies[0].wait()
    copies[1].wait()
    write_exports(field_ref, export_ref, face_ref, outs)
    for copy in copies[2:]:
        copy.wait()


def multiply(vector_ref, got_refs, diagonal_ref, coeff_ref, neighbour_ref, halo_ref, out_ref):
    group = lax.axis_index("group")
    last = lax.axis_size("group") - 1
    far, over, under, near = got_refs
    for axis, d, first, second in (("dom", 0, near, far), ("group", 2, over, under)):
        even = is_even(axis)
        below = jnp.where(even, second[...], first[...])
        above = jnp.where(even, first[...], second[...])
        if axis == "group":
            below = jnp.where(group > 0, below, 0.0)
            above = jnp.where(group < last, above, 0.0)
        halo_ref[d * FACE_ROWS : (d + 1) * FACE_ROWS, :] = below
        halo_ref[(d + 1) * FACE_ROWS : (d + 2) * FACE_ROWS, :] = above
    table = rows_of(vector_ref, ROWS) + rows_of(halo_ref, 4 * FACE_ROWS)
    for t in range(ROWS):
        cut, row = slice(t * LANES, (t + 1) * LANES), slice(t, t + 1)
        (found,) = look_up([table], neighbour_ref[:, cut])
        linked = jnp.sum(coeff_ref[:, cut] * found, axis=0, keepdims=True)
        out_ref[row, :] = diagonal_ref[row, :] * vector_ref[row, :] - linked


def first_kernel(
    pressure_ref, got0, got1, got2, got3, source_ref, diagonal_ref, coeff_ref, neighbour_ref,
    export_ref, residual_ref, direction_ref, out0, out1, out2, out3, halo_ref, product_ref, face_ref,
):
    multiply(
        pressure_ref, (got0, got1, got2, got3), diagonal_ref, coeff_ref, neighbour_ref,
        halo_ref, product_ref,
    )
    residual = source_ref[...] - product_ref[...]
    residual_ref[...] = residual
    direction_ref[...] = residual / CENTRE
    write_exports(direction_ref, export_ref, face_ref, (out0, out1, out2, out3))


def second_kernel(
    direction_ref, got0, got1, got2, got3, pressure_ref, residual_ref, diagonal_ref, coeff_ref,
    neighbour_ref, parcel_ref, moved_ref, out_ref, answer_ref, halo_ref, product_ref,
):
    multiply(
        direction_ref, (got0, got1, got2, got3), diagonal_ref, coeff_ref, neighbour_ref,
        halo_ref, product_ref,
    )
    direction = direction_ref[...]
    residual = residual_ref[...] - product_ref[...]
    iterate = pressure_ref[...] + direction
    direction = RHO_NEXT * RHO_FIRST * direction + (2.0 * RHO_NEXT / HALF_WIDTH) * residual
    out_ref[...] = iterate + direction
    table = rows_of(out_ref, ROWS)
    for s in range(OWNERS):
        (found,) = look_up([table], parcel_ref[s, 8:16, :].astype(I32))
        answer_ref[s, 0:8, :] = found
        answer_ref[s, 8:16, :] = moved_ref[s]


def send_out(local_ref, hbm_ref, sems, part):
    block = pl.ds(part * PART, PART)
    return pltpu.make_async_copy(local_ref.at[block], hbm_ref.at[block], sems.at[part])


def slot_kernel(
    owner_ref, cells_ref, weight_ref, velocity_ref, rate_ref, place_ref, sent_hbm, sent_ref,
    state_ref, sems,
):
    owners = lax.broadcasted_iota(I32, (OWNERS, LANES), 0)
    lanes = lax.broadcasted_iota(I32, (OWNERS, LANES), 1)
    chosen = [owners == wide(owner_ref[j : j + 1, :], OWNERS) for j in range(CHUNKS)]
    stacked = jnp.concatenate([c.astype(F32).astype(BF16) for c in chosen], axis=0)
    row = lax.broadcasted_iota(I32, (LANES, 2 * LANES), 0)
    column = lax.broadcasted_iota(I32, (LANES, 2 * LANES), 1)
    before = ((row < column) | (column >= LANES)).astype(F32).astype(BF16)
    counts = jnp.dot(stacked, before, preferred_element_type=F32)
    carried = jnp.zeros((OWNERS, LANES), F32)
    ranks = []
    for j in range(CHUNKS):
        part = counts[j * OWNERS : (j + 1) * OWNERS]
        rank = jnp.where(chosen[j], part[:, :LANES] + carried, 0.0)
        ranks.append(jnp.sum(rank, axis=0, keepdims=True))
        carried = carried + part[:, LANES:]
        place_ref[j : j + 1, :] = owner_ref[j : j + 1, :] * CAP + ranks[j].astype(I32)
    slots = lax.broadcasted_iota(I32, (CAP, LANES), 0).astype(F32)
    at_rank = jnp.concatenate(
        [(slots == wide(ranks[j], CAP)).astype(F32).astype(BF16) for j in range(CHUNKS)], axis=1
    )
    lane_of = jnp.concatenate(
        [jnp.where(c, lanes.astype(F32), 0.0).astype(BF16) for c in chosen], axis=1
    )
    chunk_of = jnp.concatenate(
        [jnp.where(c, F32(j + 1), 0.0).astype(BF16) for j, c in enumerate(chosen)], axis=1
    )
    found = lax.dot_general(
        jnp.concatenate([lane_of, chunk_of], axis=0), at_rank, (((1,), (1,)), ((), ())),
        preferred_element_type=F32,
    ).astype(I32)
    state_ref[0:3, :] = velocity_ref[...]
    for j in range(CHUNKS):
        state_ref[3:4, j * LANES : (j + 1) * LANES] = rate_ref[j : j + 1, :]
    state_ref[4:8, :] = jnp.zeros((4, PARCELS), F32)
    for o in range(OWNERS):
        low = wide(found[o : o + 1], 8)
        high = wide(found[OWNERS + o : OWNERS + o + 1], 8)
        here = [high == j + 1 for j in range(CHUNKS)]

        def place(ref):
            value = jnp.zeros((8, LANES), F32)
            for j in range(CHUNKS):
                part = ref[:, j * LANES : (j + 1) * LANES].astype(F32)
                value = jnp.where(here[j], pick(part, low), value)
            return value

        sent_ref[o, 0:8, :] = place(weight_ref)
        sent_ref[o, 8:16, :] = place(cells_ref)
        sent_ref[o, 16:24, :] = place(state_ref)
        if o % PART == PART - 1:
            send_out(sent_ref, sent_hbm, sems, o // PART).start()
    for part in range(OWNERS // PART):
        send_out(sent_ref, sent_hbm, sems, part).wait()


def fluid_kernel(fluid_ref, parcel_ref, moved_ref, force_ref):
    tables = [
        [lambda c=c, r=r: fluid_ref[c : c + 1, r * LANES : (r + 1) * LANES] for r in range(ROWS)]
        for c in range(3)
    ]
    for s in range(OWNERS):
        found = look_up(tables, parcel_ref[s, 8:16, :].astype(I32))
        weights = parcel_ref[s, 0:8, :]
        rate = parcel_ref[s, 19:20, :]
        for c in range(3):
            velocity = parcel_ref[s, 16 + c : 17 + c, :]
            fluid_at = jnp.sum(weights * found[c], axis=0, keepdims=True)
            moved_ref[s, c : c + 1, :] = velocity + rate * (fluid_at - velocity)
            force_ref[s, c : c + 1, :] = rate * (velocity - fluid_at)
        moved_ref[s, 3:8, :] = jnp.zeros((5, LANES), F32)
        force_ref[s, 3:4, :] = jnp.zeros((1, LANES), F32)


def scatter_kernel(parcel_ref, force_ref, out_ref, total_ref):
    rows = lax.broadcasted_iota(I32, (ROWS, LANES), 0)
    columns = lax.broadcasted_iota(I32, (LANES, LANES), 0)
    total_ref[...] = jnp.zeros_like(total_ref)
    for first in range(0, OWNERS, 4):
        left, right = [], []
        for s in range(first, first + 4):
            cells = parcel_ref[s, 8:16, :].astype(I32)
            high = lax.shift_right_logical(cells, 7)
            low = lax.bitwise_and(cells, 127)
            weights = LOADING * parcel_ref[s, 0:8, :]
            parts = []
            for c in range(3):
                value = weights * force_ref[s, c : c + 1, :]
                top = value.astype(BF16).astype(F32)
                parts.append(top)
                parts.append(value - top)
            for k in range(K):
                here = rows == wide(high[k : k + 1], ROWS)
                chosen = [jnp.where(here, wide(p[k : k + 1], ROWS), 0.0).astype(BF16) for p in parts]
                left.append(jnp.concatenate(chosen, axis=0))
                right.append((columns == wide(low[k : k + 1], LANES)).astype(F32).astype(BF16))
        total_ref[...] += lax.dot_general(
            jnp.concatenate(left, axis=1), jnp.concatenate(right, axis=1),
            (((1,), (1,)), ((), ())), preferred_element_type=F32,
        )
    for c in range(3):
        both = (
            total_ref[2 * c * ROWS : (2 * c + 1) * ROWS, :]
            + total_ref[(2 * c + 1) * ROWS : (2 * c + 2) * ROWS, :]
        )
        for r in range(ROWS):
            out_ref[c : c + 1, r * LANES : (r + 1) * LANES] = both[r : r + 1]


def return_kernel(place_ref, answer_ref, grad_ref, out_ref):
    for j in range(CHUNKS):
        cut = slice(j * LANES, (j + 1) * LANES)
        place = wide(place_ref[j : j + 1, :], 8)
        high = lax.shift_right_logical(place, 7)
        low = lax.bitwise_and(place, 127)
        pressure = jnp.zeros((8, LANES), F32)
        moved = jnp.zeros((8, LANES), F32)
        for o in range(OWNERS):
            here = high == o
            pressure = jnp.where(here, pick(answer_ref[o, 0:8, :], low), pressure)
            moved = jnp.where(here, pick(answer_ref[o, 8:16, :], low), moved)
        for c in range(3):
            gradient = jnp.sum(grad_ref[c, :, cut] * pressure, axis=0, keepdims=True)
            out_ref[c : c + 1, cut] = moved[c : c + 1] - gradient


def shape(*dims, dtype=F32):
    return jax.ShapeDtypeStruct(dims, dtype)


def exchange(faces):
    groups, count = lax.axis_size("group"), lax.axis_size("dom")
    near = [(m, m ^ 1) for m in range(count)]
    far = [(m, (m - 1 if m % 2 == 0 else m + 1) % count) for m in range(count)]
    over = [(g, g ^ 1) for g in range(groups)]
    under = []
    for g in range(groups):
        to = g - 1 if g % 2 == 0 else g + 1
        for m in range(count):
            inside = 0 <= to < groups
            under.append((g * count + m, to * count + m if inside else g * count + (m ^ 1)))
    return (
        lax.ppermute(faces[0], "dom", far),
        lax.ppermute(faces[1], "group", over),
        lax.ppermute(faces[2], ("group", "dom"), under),
        lax.ppermute(faces[3], "dom", near),
    )


def call(kernel, outs, flops, scratch=(), grant=32, **kwargs):
    return pl.pallas_call(
        kernel,
        out_shape=outs,
        scratch_shapes=list(scratch),
        compiler_params=pltpu.CompilerParams(vmem_limit_bytes=grant * 1024 * 1024),
        cost_estimate=pl.CostEstimate(flops=flops, bytes_accessed=400000, transcendentals=0),
        **kwargs,
    )


def per_device(
    pressure_old, source_term, diagonal, face_coeffs, neighbours, export_cells, fluid_velocity,
    parcel_velocity, drag_rate, parcel_owner, parcel_cells, interp_weights, grad_weights,
):
    pressure_old = pressure_old.reshape(ROWS, LANES)
    source_term = source_term.reshape(ROWS, LANES)
    diagonal = diagonal.reshape(ROWS, LANES)
    face = shape(FACE_ROWS, LANES)
    field = shape(ROWS, LANES)
    faces_buffer = pltpu.VMEM((4, FACE_ROWS, LANES), F32)
    halo = (pltpu.VMEM((4 * FACE_ROWS, LANES), F32), pltpu.VMEM((ROWS, LANES), F32))

    kept = [
        pltpu.with_memory_space_constraint(x, pltpu.HBM)
        for x in (
            pressure_old, export_cells, parcel_owner.reshape(CHUNKS, LANES), parcel_cells,
            interp_weights, parcel_velocity, drag_rate.reshape(CHUNKS, LANES),
        )
    ]
    outs = call(
        export_kernel,
        (face,) * 4 + tuple(shape(*x.shape, dtype=x.dtype) for x in kept[2:]),
        10**6,
        (
            faces_buffer, pltpu.VMEM((ROWS, LANES), F32), pltpu.VMEM((4, FACE), I32),
            pltpu.SemaphoreType.DMA((len(kept),)),
        ),
        in_specs=[pl.BlockSpec(memory_space=pltpu.HBM)] * len(kept),
    )(*kept)
    got = exchange(outs[:4])
    everything = pl.BlockSpec(memory_space=pltpu.VMEM)
    outside = pl.BlockSpec(memory_space=pl.ANY)
    parts = pltpu.SemaphoreType.DMA((OWNERS // PART,))
    place, sent = call(
        slot_kernel, (shape(CHUNKS, LANES, dtype=I32), shape(OWNERS, SENT, CAP)), 10**8,
        (pltpu.VMEM((OWNERS, SENT, CAP), F32), pltpu.VMEM((8, PARCELS), F32), parts),
        out_specs=(everything, outside),
    )(*outs[4:])
    got, sent = lax.optimization_barrier((got, sent))
    parcels = lax.all_to_all(sent, "dom", split_axis=0, concat_axis=0, tiled=True)
    residual, direction, *faces = call(
        first_kernel, (field, field) + (face,) * 4, 10**8,
        halo + (faces_buffer,),
    )(pressure_old, *got, source_term, diagonal, face_coeffs, neighbours, export_cells)
    got = exchange(faces)
    moved, force = call(
        fluid_kernel, (shape(OWNERS, 8, CAP), shape(OWNERS, 4, CAP)), 10**9
    )(fluid_velocity, parcels)
    iterate, answer = call(second_kernel, (field, shape(OWNERS, BACK, CAP)), 10**8, halo)(
        direction, *got, pressure_old, residual, diagonal, face_coeffs, neighbours, parcels, moved
    )
    returned = lax.all_to_all(answer, "dom", split_axis=0, concat_axis=0, tiled=True)
    momentum_source = call(
        scatter_kernel, shape(3, CELLS), 2 * 10**9, (pltpu.VMEM((6 * ROWS, LANES), F32),)
    )(parcels, force)
    parcel_new = call(return_kernel, shape(3, PARCELS), 10**6)(place, returned, grad_weights)
    return (iterate.reshape(CELLS), parcel_new, momentum_source)


def solution(mesh):
    whole = ("group", "dom")
    flat, rows = P(whole), P(None, whole)
    return jax.shard_map(
        per_device,
        mesh=mesh,
        in_specs=(
            flat, flat, flat, rows, rows, rows, rows, rows, flat, flat, rows, rows,
            P(None, None, whole),
        ),
        out_specs=(flat, rows, rows),
        check_vma=False,
    )
```

```python
import jax
import jax.numpy as jnp
from jax import lax
from jax.experimental import pallas as pl
from jax.experimental.pallas import tpu as pltpu
from jax.sharding import PartitionSpec as P

CENTRE = 7.0
HALF_WIDTH = 4.0
LOADING = 8.0
SIGMA = CENTRE / HALF_WIDTH
RHO_FIRST = 1.0 / SIGMA
RHO_NEXT = 1.0 / (2.0 * SIGMA - RHO_FIRST)

CELLS = 4096
LANES = 128
ROWS = CELLS // LANES
FACE = 1024
FACE_ROWS = FACE // LANES
NBR = 6
K = 8
PARCELS = 1024
CHUNKS = PARCELS // LANES
OWNERS = 32
CAP = 128
SENT = 24
BACK = 16

F32 = jnp.float32
BF16 = jnp.bfloat16
I32 = jnp.int32


def pick(row, lanes):
    return jnp.take_along_axis(row, lanes, axis=1, mode="promise_in_bounds")


def wide(row, height):
    return jnp.broadcast_to(row, (height, LANES))


def look_up(tables, index):
    height = index.shape[0]
    high = lax.shift_right_logical(index, 7)
    low = lax.bitwise_and(index, 127)
    found = [jnp.zeros((height, LANES), F32) for _ in tables]
    for r in range(len(tables[0])):
        here = high == r
        for c, table in enumerate(tables):
            found[c] = jnp.where(here, pick(wide(table[r](), height), low), found[c])
    return found


def rows_of(ref, count):
    return [lambda r=r: ref[r : r + 1, :] for r in range(count)]


def is_even(axis):
    return lax.rem(lax.axis_index(axis), 2) == 0


def write_exports(field_ref, export_ref, face_ref, outs):
    for t in range(FACE_ROWS):
        index = export_ref[:, t * LANES : (t + 1) * LANES]
        (found,) = look_up([rows_of(field_ref, ROWS)], index)
        for d in range(4):
            face_ref[d, t : t + 1, :] = found[d : d + 1]
    for axis, d, first, second in (("dom", 0, outs[3], outs[0]), ("group", 2, outs[1], outs[2])):
        even = is_even(axis)
        first[...] = jnp.where(even, face_ref[d], face_ref[d + 1])
        second[...] = jnp.where(even, face_ref[d + 1], face_ref[d])


def export_kernel(*refs):
    (field_hbm, export_hbm), passed = refs[:2], refs[2:7]
    outs, passed_on = refs[7:11], refs[11:16]
    face_ref, field_ref, export_ref, sems = refs[16:]
    sources = (field_hbm, export_hbm) + passed
    targets = (field_ref, export_ref) + passed_on
    copies = [
        pltpu.make_async_copy(source, target, sems.at[i])
        for i, (source, target) in enumerate(zip(sources, targets))
    ]
    for copy in copies:
        copy.start()
    copies[0].wait()
    copies[1].wait()
    write_exports(field_ref, export_ref, face_ref, outs)
    for copy in copies[2:]:
        copy.wait()


def multiply(vector_ref, got_refs, diagonal_ref, coeff_ref, neighbour_ref, halo_ref, out_ref):
    group = lax.axis_index("group")
    last = lax.axis_size("group") - 1
    far, over, under, near = got_refs
    for axis, d, first, second in (("dom", 0, near, far), ("group", 2, over, under)):
        even = is_even(axis)
        below = jnp.where(even, second[...], first[...])
        above = jnp.where(even, first[...], second[...])
        if axis == "group":
            below = jnp.where(group > 0, below, 0.0)
            above = jnp.where(group < last, above, 0.0)
        halo_ref[d * FACE_ROWS : (d + 1) * FACE_ROWS, :] = below
        halo_ref[(d + 1) * FACE_ROWS : (d + 2) * FACE_ROWS, :] = above
    table = rows_of(vector_ref, ROWS) + rows_of(halo_ref, 4 * FACE_ROWS)
    for t in range(ROWS):
        cut, row = slice(t * LANES, (t + 1) * LANES), slice(t, t + 1)
        (found,) = look_up([table], neighbour_ref[:, cut])
        linked = jnp.sum(coeff_ref[:, cut] * found, axis=0, keepdims=True)
        out_ref[row, :] = diagonal_ref[row, :] * vector_ref[row, :] - linked


def first_kernel(
    pressure_ref, got0, got1, got2, got3, source_ref, diagonal_ref, coeff_ref, neighbour_ref,
    export_ref, residual_ref, direction_ref, out0, out1, out2, out3, halo_ref, product_ref, face_ref,
):
    multiply(
        pressure_ref, (got0, got1, got2, got3), diagonal_ref, coeff_ref, neighbour_ref,
        halo_ref, product_ref,
    )
    residual = source_ref[...] - product_ref[...]
    residual_ref[...] = residual
    direction_ref[...] = residual / CENTRE
    write_exports(direction_ref, export_ref, face_ref, (out0, out1, out2, out3))


def second_kernel(
    direction_ref, got0, got1, got2, got3, pressure_ref, residual_ref, diagonal_ref, coeff_ref,
    neighbour_ref, parcel_ref, moved_ref, out_ref, answer_ref, halo_ref, product_ref,
):
    multiply(
        direction_ref, (got0, got1, got2, got3), diagonal_ref, coeff_ref, neighbour_ref,
        halo_ref, product_ref,
    )
    direction = direction_ref[...]
    residual = residual_ref[...] - product_ref[...]
    iterate = pressure_ref[...] + direction
    direction = RHO_NEXT * RHO_FIRST * direction + (2.0 * RHO_NEXT / HALF_WIDTH) * residual
    out_ref[...] = iterate + direction
    table = rows_of(out_ref, ROWS)
    for s in range(OWNERS):
        (found,) = look_up([table], parcel_ref[s, 8:16, :].astype(I32))
        answer_ref[s, 0:8, :] = found
        answer_ref[s, 8:16, :] = moved_ref[s]


def slot_kernel(
    owner_ref, cells_ref, weight_ref, velocity_ref, rate_ref, place_ref, sent_ref,
    state_ref,
):
    owners = lax.broadcasted_iota(I32, (OWNERS, LANES), 0)
    lanes = lax.broadcasted_iota(I32, (OWNERS, LANES), 1)
    chosen = [owners == wide(owner_ref[j : j + 1, :], OWNERS) for j in range(CHUNKS)]
    stacked = jnp.concatenate([c.astype(F32).astype(BF16) for c in chosen], axis=0)
    row = lax.broadcasted_iota(I32, (LANES, 2 * LANES), 0)
    column = lax.broadcasted_iota(I32, (LANES, 2 * LANES), 1)
    before = ((row < column) | (column >= LANES)).astype(F32).astype(BF16)
    counts = jnp.dot(stacked, before, preferred_element_type=F32)
    carried = jnp.zeros((OWNERS, LANES), F32)
    ranks = []
    for j in range(CHUNKS):
        part = counts[j * OWNERS : (j + 1) * OWNERS]
        rank = jnp.where(chosen[j], part[:, :LANES] + carried, 0.0)
        ranks.append(jnp.sum(rank, axis=0, keepdims=True))
        carried = carried + part[:, LANES:]
        place_ref[j : j + 1, :] = owner_ref[j : j + 1, :] * CAP + ranks[j].astype(I32)
    slots = lax.broadcasted_iota(I32, (CAP, LANES), 0).astype(F32)
    at_rank = jnp.concatenate(
        [(slots == wide(ranks[j], CAP)).astype(F32).astype(BF16) for j in range(CHUNKS)], axis=1
    )
    lane_of = jnp.concatenate(
        [jnp.where(c, lanes.astype(F32), 0.0).astype(BF16) for c in chosen], axis=1
    )
    chunk_of = jnp.concatenate(
        [jnp.where(c, F32(j + 1), 0.0).astype(BF16) for j, c in enumerate(chosen)], axis=1
    )
    found = lax.dot_general(
        jnp.concatenate([lane_of, chunk_of], axis=0), at_rank, (((1,), (1,)), ((), ())),
        preferred_element_type=F32,
    ).astype(I32)
    state_ref[0:3, :] = velocity_ref[...]
    for j in range(CHUNKS):
        state_ref[3:4, j * LANES : (j + 1) * LANES] = rate_ref[j : j + 1, :]
    state_ref[4:8, :] = jnp.zeros((4, PARCELS), F32)
    for o in range(OWNERS):
        low = wide(found[o : o + 1], 8)
        high = wide(found[OWNERS + o : OWNERS + o + 1], 8)
        here = [high == j + 1 for j in range(CHUNKS)]

        def place(ref):
            value = jnp.zeros((8, LANES), F32)
            for j in range(CHUNKS):
                part = ref[:, j * LANES : (j + 1) * LANES].astype(F32)
                value = jnp.where(here[j], pick(part, low), value)
            return value

        sent_ref[o, 0:8, :] = place(weight_ref)
        sent_ref[o, 8:16, :] = place(cells_ref)
        sent_ref[o, 16:24, :] = place(state_ref)


def fluid_kernel(fluid_ref, parcel_ref, moved_ref, force_ref):
    tables = [
        [lambda c=c, r=r: fluid_ref[c : c + 1, r * LANES : (r + 1) * LANES] for r in range(ROWS)]
        for c in range(3)
    ]
    for s in range(OWNERS):
        found = look_up(tables, parcel_ref[s, 8:16, :].astype(I32))
        weights = parcel_ref[s, 0:8, :]
        rate = parcel_ref[s, 19:20, :]
        for c in range(3):
            velocity = parcel_ref[s, 16 + c : 17 + c, :]
            fluid_at = jnp.sum(weights * found[c], axis=0, keepdims=True)
            moved_ref[s, c : c + 1, :] = velocity + rate * (fluid_at - velocity)
            force_ref[s, c : c + 1, :] = rate * (velocity - fluid_at)
        moved_ref[s, 3:8, :] = jnp.zeros((5, LANES), F32)
        force_ref[s, 3:4, :] = jnp.zeros((1, LANES), F32)


def scatter_kernel(parcel_ref, force_ref, out_ref, total_ref):
    rows = lax.broadcasted_iota(I32, (ROWS, LANES), 0)
    columns = lax.broadcasted_iota(I32, (LANES, LANES), 0)
    total_ref[...] = jnp.zeros_like(total_ref)
    for first in range(0, OWNERS, 4):
        left, right = [], []
        for s in range(first, first + 4):
            cells = parcel_ref[s, 8:16, :].astype(I32)
            high = lax.shift_right_logical(cells, 7)
            low = lax.bitwise_and(cells, 127)
            weights = LOADING * parcel_ref[s, 0:8, :]
            parts = []
            for c in range(3):
                value = weights * force_ref[s, c : c + 1, :]
                top = value.astype(BF16).astype(F32)
                parts.append(top)
                parts.append(value - top)
            for k in range(K):
                here = rows == wide(high[k : k + 1], ROWS)
                chosen = [jnp.where(here, wide(p[k : k + 1], ROWS), 0.0).astype(BF16) for p in parts]
                left.append(jnp.concatenate(chosen, axis=0))
                right.append((columns == wide(low[k : k + 1], LANES)).astype(F32).astype(BF16))
        total_ref[...] += lax.dot_general(
            jnp.concatenate(left, axis=1), jnp.concatenate(right, axis=1),
            (((1,), (1,)), ((), ())), preferred_element_type=F32,
        )
    for c in range(3):
        both = (
            total_ref[2 * c * ROWS : (2 * c + 1) * ROWS, :]
            + total_ref[(2 * c + 1) * ROWS : (2 * c + 2) * ROWS, :]
        )
        for r in range(ROWS):
            out_ref[c : c + 1, r * LANES : (r + 1) * LANES] = both[r : r + 1]


def return_kernel(place_ref, answer_ref, grad_ref, out_ref):
    for j in range(CHUNKS):
        cut = slice(j * LANES, (j + 1) * LANES)
        place = wide(place_ref[j : j + 1, :], 8)
        high = lax.shift_right_logical(place, 7)
        low = lax.bitwise_and(place, 127)
        pressure = jnp.zeros((8, LANES), F32)
        moved = jnp.zeros((8, LANES), F32)
        for o in range(OWNERS):
            here = high == o
            pressure = jnp.where(here, pick(answer_ref[o, 0:8, :], low), pressure)
            moved = jnp.where(here, pick(answer_ref[o, 8:16, :], low), moved)
        for c in range(3):
            gradient = jnp.sum(grad_ref[c, :, cut] * pressure, axis=0, keepdims=True)
            out_ref[c : c + 1, cut] = moved[c : c + 1] - gradient


def shape(*dims, dtype=F32):
    return jax.ShapeDtypeStruct(dims, dtype)


def exchange(faces):
    groups, count = lax.axis_size("group"), lax.axis_size("dom")
    near = [(m, m ^ 1) for m in range(count)]
    far = [(m, (m - 1 if m % 2 == 0 else m + 1) % count) for m in range(count)]
    over = [(g, g ^ 1) for g in range(groups)]
    under = []
    for g in range(groups):
        to = g - 1 if g % 2 == 0 else g + 1
        for m in range(count):
            inside = 0 <= to < groups
            under.append((g * count + m, to * count + m if inside else g * count + (m ^ 1)))
    return (
        lax.ppermute(faces[0], "dom", far),
        lax.ppermute(faces[1], "group", over),
        lax.ppermute(faces[2], ("group", "dom"), under),
        lax.ppermute(faces[3], "dom", near),
    )


def call(kernel, outs, flops, scratch=(), grant=32, **kwargs):
    return pl.pallas_call(
        kernel,
        out_shape=outs,
        scratch_shapes=list(scratch),
        compiler_params=pltpu.CompilerParams(vmem_limit_bytes=grant * 1024 * 1024),
        cost_estimate=pl.CostEstimate(flops=flops, bytes_accessed=400000, transcendentals=0),
        **kwargs,
    )


def per_device(
    pressure_old, source_term, diagonal, face_coeffs, neighbours, export_cells, fluid_velocity,
    parcel_velocity, drag_rate, parcel_owner, parcel_cells, interp_weights, grad_weights,
):
    pressure_old = pressure_old.reshape(ROWS, LANES)
    source_term = source_term.reshape(ROWS, LANES)
    diagonal = diagonal.reshape(ROWS, LANES)
    face = shape(FACE_ROWS, LANES)
    field = shape(ROWS, LANES)
    faces_buffer = pltpu.VMEM((4, FACE_ROWS, LANES), F32)
    halo = (pltpu.VMEM((4 * FACE_ROWS, LANES), F32), pltpu.VMEM((ROWS, LANES), F32))

    kept = [
        pltpu.with_memory_space_constraint(x, pltpu.HBM)
        for x in (
            pressure_old, export_cells, parcel_owner.reshape(CHUNKS, LANES), parcel_cells,
            interp_weights, parcel_velocity, drag_rate.reshape(CHUNKS, LANES),
        )
    ]
    outs = call(
        export_kernel,
        (face,) * 4 + tuple(shape(*x.shape, dtype=x.dtype) for x in kept[2:]),
        10**6,
        (
            faces_buffer, pltpu.VMEM((ROWS, LANES), F32), pltpu.VMEM((4, FACE), I32),
            pltpu.SemaphoreType.DMA((len(kept),)),
        ),
        in_specs=[pl.BlockSpec(memory_space=pltpu.HBM)] * len(kept),
    )(*kept)
    got = exchange(outs[:4])
    place, sent = call(
        slot_kernel, (shape(CHUNKS, LANES, dtype=I32), shape(OWNERS, SENT, CAP)), 10**8,
        (pltpu.VMEM((8, PARCELS), F32),),
    )(*outs[4:])
    got, sent = lax.optimization_barrier((got, sent))
    parcels = lax.all_to_all(sent, "dom", split_axis=0, concat_axis=0, tiled=True)
    residual, direction, *faces = call(
        first_kernel, (field, field) + (face,) * 4, 10**8,
        halo + (faces_buffer,),
    )(pressure_old, *got, source_term, diagonal, face_coeffs, neighbours, export_cells)
    got = exchange(faces)
    moved, force = call(
        fluid_kernel, (shape(OWNERS, 8, CAP), shape(OWNERS, 4, CAP)), 10**9
    )(fluid_velocity, parcels)
    iterate, answer = call(second_kernel, (field, shape(OWNERS, BACK, CAP)), 10**8, halo)(
        direction, *got, pressure_old, residual, diagonal, face_coeffs, neighbours, parcels, moved
    )
    returned = lax.all_to_all(answer, "dom", split_axis=0, concat_axis=0, tiled=True)
    momentum_source = call(
        scatter_kernel, shape(3, CELLS), 2 * 10**9, (pltpu.VMEM((6 * ROWS, LANES), F32),)
    )(parcels, force)
    parcel_new = call(return_kernel, shape(3, PARCELS), 10**6)(place, returned, grad_weights)
    return (iterate.reshape(CELLS), parcel_new, momentum_source)


def solution(mesh):
    whole = ("group", "dom")
    flat, rows = P(whole), P(None, whole)
    return jax.shard_map(
        per_device,
        mesh=mesh,
        in_specs=(
            flat, flat, flat, rows, rows, rows, rows, rows, flat, flat, rows, rows,
            P(None, None, whole),
        ),
        out_specs=(flat, rows, rows),
        check_vma=False,
    )
```
